128 devices in a mesh: row: 8 (over x_hi, z), col: 16 (over y, x_lo, core).
Axes of the slice: x: 4 (x_hi: 2, x_lo: 2; x = x_hi * 2 + x_lo), y: 4, z: 4, core: 2. Of those that a mesh axis runs over, the one named last changes fastest.
Arguments:
- root_front: float32 [8192, 8192], P('row', 'col'), may hold values from -0.03314563 to 10.033146, as said below
- contrib: float32 [16384, 4096], P('row', 'col'), may hold values from -0.046875 to 0.046875, as said below
- index_map: int32 [4, 4096], replicated, may hold values from 0 to 8191, as said below
Outputs:
- factored: float32 [8192, 8192], P('row', 'col')
The draws below stay inside these ranges and needn't reach their ends.
Inputs may be any that keep to these rules, and one draw needn't show every extreme that they name: `index_map`: each child's list is strictly increasing, and exactly 256 of its entries lie in each range [j * 512, (j + 1) * 512). `root_front`: Symmetric, and positive definite after the children's blocks are added. `contrib`: each child's update matrix is symmetric.
All inputs are finite; a program needn't handle non-finite values.
Results may differ from the reference program's by a relative error of at most 0.0001.
Values sent between devices are 32-bit elements; how exact they have to be, the bound alone decides.
No kernel may reach another device: no remote copies, remote signals or barrier semaphores. Data moves between devices by JAX's collectives and lax.ppermute only.
A program may use at most 128 MiB of HBM per device.

```python
import jax
import jax.numpy as jnp
from jax import lax

NF = 8192
CB = 4096
NKIDS = 4
BLOCK = 512
PANELS = 3
RANGE = 512
PICK = 256
GROUP = 2
CYC = 256


def symmetric_noise(key, shape, scale):
    values = jax.random.truncated_normal(key, -4.0, 4.0, shape, jnp.float32)
    return (values + jnp.swapaxes(values, -1, -2)) * (scale * 0.70710678)


def draw_root_front(key, part):
    key = jax.random.fold_in(key, 11)
    key_noise, key_diag = jax.random.split(key)
    positions = jnp.arange(NF)
    distance = jnp.abs(positions[:, None] - positions[None, :]).astype(jnp.float32)
    coupling = 2.0 * jnp.power(0.98, distance)
    noise = symmetric_noise(key_noise, (NF, NF), 0.5 / NF ** 0.5)
    unit = jax.random.uniform(key_diag, (NF,), jnp.float32)
    extra = jnp.exp(jnp.log(4.0) + unit * jnp.log(2.0))
    is_diag = positions[:, None] == positions[None, :]
    return coupling + noise + jnp.where(is_diag, extra[:, None], 0.0)


def draw_contrib(key, part):
    key = jax.random.fold_in(key, 12)
    noise = symmetric_noise(key, (NKIDS, CB, CB), 0.5 / CB ** 0.5)
    stored = noise.reshape(NKIDS, CB // (GROUP * CYC), GROUP, CYC, CB).transpose(0, 2, 1, 3, 4)
    return stored.reshape(NKIDS * CB, CB)


def draw_index_map(key, part):
    key = jax.random.fold_in(key, 13)
    ranges = NF // RANGE
    keys = jax.random.split(key, NKIDS * ranges)
    picks = jax.vmap(lambda one_key: jnp.sort(jax.random.permutation(one_key, RANGE)[:PICK]))(keys)
    offsets = jnp.arange(ranges, dtype=jnp.int32) * RANGE
    picks = picks.reshape(NKIDS, ranges, PICK) + offsets[None, :, None]
    return picks.reshape(NKIDS, CB).astype(jnp.int32)


def setup_inputs(seed: int = 0) -> dict:
    splits = jax.random.split(jax.random.key(seed), 4)
    root_front = draw_root_front(jax.random.fold_in(splits[3], 71), 0)
    contrib = draw_contrib(jax.random.fold_in(splits[3], 71), 0)
    index_map = draw_index_map(jax.random.fold_in(splits[3], 71), 0)
    return dict(root_front=root_front, contrib=contrib, index_map=index_map)


def reference(root_front, contrib, index_map):
    assembled = root_front
    for child_id in range(NKIDS):
        child_rows = index_map[child_id]
        stored = contrib[child_id * CB:(child_id + 1) * CB]
        child_block = stored.reshape(GROUP, CB // (GROUP * CYC), CYC, CB).transpose(1, 0, 2, 3).reshape(CB, CB)
        assembled = assembled.at[child_rows[:, None], child_rows[None, :]].add(child_block)
    for panel_step in range(PANELS):
        col_start = panel_step * BLOCK
        col_end = col_start + BLOCK
        pivot_factor = jnp.linalg.cholesky(assembled[col_start:col_end, col_start:col_end])
        solved = lax.linalg.triangular_solve(pivot_factor, assembled[col_end:, col_start:col_end], left_side=False, lower=True, transpose_a=True)
        schur = assembled[col_end:, col_end:] - jnp.dot(solved.astype(jnp.float32), solved.T.astype(jnp.float32), precision=lax.Precision.HIGHEST, preferred_element_type=jnp.float32)
        assembled = assembled.at[col_end:, col_end:].set(schur)
        assembled = assembled.at[col_start:col_end, col_start:col_end].set(pivot_factor)
        assembled = assembled.at[col_end:, col_start:col_end].set(solved)
        assembled = assembled.at[col_start:col_end, col_end:].set(0.0)
    return assembled
```

```python
import functools

import jax
import jax.numpy as jnp
from jax import lax
from jax.experimental import pallas as pl
from jax.experimental.pallas import tpu as pltpu
from jax.sharding import PartitionSpec as P

CB = 4096
NKIDS = 4
BLOCK = 512
PANELS = 3
PICK = 256
LEAD = BLOCK * PANELS
F32 = jnp.float32
B16 = jnp.bfloat16


def split3(x):
    high = x.astype(B16).astype(F32)
    rest = x - high
    mid = rest.astype(B16).astype(F32)
    return high, mid, rest - mid


def outer_update(lhs, rhs):
    a_high, a_mid, a_low = split3(lhs)
    b_high, b_mid, b_low = split3(rhs)
    a = jnp.concatenate([a_high, a_high, a_mid, a_high, a_low, a_mid], 0).astype(B16)
    b = jnp.concatenate([b_high, b_mid, b_high, b_low, b_high, b_mid], 0).astype(B16)
    return lax.dot_general(a, b, (((0,), (0,)), ((), ())), preferred_element_type=F32)


def factor_tile(rows):
    count = len(rows)
    lane = lax.broadcasted_iota(jnp.int32, (8, 128), 1)
    sub = lax.broadcasted_iota(jnp.int32, (8, 128), 0)
    rows = list(rows)
    uppers, inverses = [], []
    for k in range(count):
        c0 = 8 * k
        own = (lane >= c0) & (lane < c0 + 8)
        cur = rows[k]
        nxt = rows[k + 1] if k + 1 < count else None
        top = [jnp.broadcast_to(cur[:, c0 + j : c0 + j + 1], (8, 128)) for j in range(8)]
        if nxt is not None:
            low = [jnp.broadcast_to(nxt[:, c0 + j : c0 + j + 1], (8, 128)) for j in range(8)]
            after = jnp.where(own, 0.0, nxt)
        upper = cur
        inv = jnp.where(own, jnp.where(lane - c0 == sub, 1.0, 0.0), cur)
        for j in range(8):
            scale = lax.rsqrt(jnp.broadcast_to(top[j][j : j + 1, :], (8, 128)))
            mult = jnp.where(sub > j, top[j] * scale, 0.0)
            if nxt is not None:
                low_mult = low[j] * scale
            for m in range(j + 1, 8):
                u = jnp.broadcast_to(top[m][j : j + 1, :], (8, 128)) * scale
                top[m] = top[m] - mult * u
                if nxt is not None:
                    low[m] = low[m] - low_mult * u
            u = jnp.broadcast_to(upper[j : j + 1, :], (8, 128)) * scale
            upper = jnp.where(sub == j, u, upper - mult * u)
            u = jnp.broadcast_to(inv[j : j + 1, :], (8, 128)) * scale
            inv = jnp.where(sub == j, u, inv - mult * u)
            if nxt is not None:
                after = after - low_mult * u
        uppers.append(jnp.where(lane - c0 >= sub, upper, 0.0))
        inverses.append(jnp.where(lane < c0 + 8, inv, 0.0))
        if nxt is not None:
            rows[k + 1] = after
        if k + 2 < count:
            update = outer_update(jnp.where(lane >= c0 + 16, upper, 0.0), inv)
            for i in range(k + 2, count):
                rows[i] = jnp.where(own, 0.0, rows[i]) - update[8 * i : 8 * i + 8, :]
    return uppers, inverses


def mm(a, b, flip=False):
    dims = (((1,), (1 if flip else 0,)), ((), ()))
    return lax.dot_general(a, b, dims, precision=lax.Precision.HIGHEST, preferred_element_type=F32)


def factor_block(l_ref, w_ref, s_ref):
    size = s_ref.shape[0]
    tiles = size // 128
    l_ref[...] = jnp.zeros_like(l_ref)
    w_ref[...] = jnp.zeros_like(w_ref)
    for k in range(tiles):
        o = 128 * k
        e = o + 128
        rows = [s_ref[o + 8 * i : o + 8 * i + 8, o:e] for i in range(16)]
        uppers, inverses = factor_tile(rows)
        inv = jnp.concatenate(inverses, 0)
        l_ref[o:e, o:e] = jnp.concatenate(uppers, 0).T
        w_ref[o:e, o:e] = inv
        if k + 1 < tiles:
            below = mm(s_ref[e:, o:e], inv, True)
            l_ref[e:, o:e] = below
            s_ref[e:, e:] = s_ref[e:, e:] - mm(below, below, True)
    half = 128
    while half < size:
        for o in range(0, size, 2 * half):
            m = o + half
            e = m + half
            t = mm(l_ref[m:e, o:m], w_ref[o:m, o:m])
            w_ref[m:e, o:m] = -mm(w_ref[m:e, m:e], t)
        half *= 2


def factor0(a_ref, l_ref, w_ref, s_ref):
    s_ref[...] = a_ref[...]
    factor_block(l_ref, w_ref, s_ref)


def factor1(a_ref, w0_ref, l_ref, w_ref, l10_ref, s_ref):
    l10 = mm(a_ref[:, :BLOCK], w0_ref[...], True)
    l10_ref[...] = l10
    s_ref[...] = a_ref[:, BLOCK:] - mm(l10, l10, True)
    factor_block(l_ref, w_ref, s_ref)


def factor2(a_ref, w0_ref, w1_ref, l10_ref, l_ref, w_ref, l20_ref, l21_ref, s_ref):
    l20 = mm(a_ref[:, :BLOCK], w0_ref[...], True)
    l20_ref[...] = l20
    l21 = mm(a_ref[:, BLOCK : 2 * BLOCK] - mm(l20, l10_ref[...], True), w1_ref[...], True)
    l21_ref[...] = l21
    s_ref[...] = a_ref[:, 2 * BLOCK :] - mm(l20, l20, True) - mm(l21, l21, True)
    factor_block(l_ref, w_ref, s_ref)


def factor_call(kernel, outs, *args):
    square = jax.ShapeDtypeStruct((BLOCK, BLOCK), F32)
    return pl.pallas_call(
        kernel,
        out_shape=[square] * outs,
        scratch_shapes=[pltpu.VMEM((BLOCK, BLOCK), F32)],
        compiler_params=pltpu.CompilerParams(vmem_limit_bytes=40 << 20),
        cost_estimate=pl.CostEstimate(flops=20_000_000_000, bytes_accessed=1 << 24, transcendentals=0),
    )(*args)


def dot3(a, b, flip=False):
    dims = (((1,), (1 if flip else 0,)), ((), ()))
    return lax.dot_general(a, b, dims, precision=lax.Precision.HIGH, preferred_element_type=F32)


def spread(a, axis, count):
    return lax.all_to_all(jnp.broadcast_to(a[None], (count,) + a.shape), axis, 0, 0, tiled=True)


def body(root_front, contrib, index_map):
    nr = lax.axis_size("row")
    nc = lax.axis_size("col")
    r = lax.axis_index("row")
    c = lax.axis_index("col")
    rows_loc, cols_loc = root_front.shape
    group = nr // NKIDS
    kid = r // group
    part = r % group
    place = jnp.arange(BLOCK, dtype=jnp.int32)

    def hot(kid_id, rng):
        own = lax.dynamic_slice(index_map, (kid_id, rng * PICK), (1, PICK))[0] - rng * BLOCK
        return (own[:, None] == place[None, :]).astype(F32)

    with jax.named_scope("slices"):
        own_cols = hot(kid, c)
        first = dot3(own_cols.T, contrib[:PICK].T)
        third = dot3(own_cols.T, contrib[PICK : 2 * PICK].T)
        first = dot3(first, hot(kid, part))
        root_t = root_front.T
        first = first + jnp.where(r == 0, root_t[:, :BLOCK], 0.0)
        second = jnp.where(r == 0, root_t[:, BLOCK:], root_t[:, :BLOCK])
        outgoing = jnp.concatenate([first, second, third], 1)
        outgoing = outgoing.reshape(nr, cols_loc // nr, 2 * BLOCK + PICK)
        got = lax.all_to_all(outgoing, "row", 0, 0, tiled=True)
        lead0 = got[0, :, :BLOCK] + got[2, :, :BLOCK] + got[4, :, :BLOCK] + got[6, :, :BLOCK]
        lead1 = got[1, :, :BLOCK] + got[3, :, :BLOCK] + got[5, :, :BLOCK] + got[7, :, :BLOCK]
        lead1 = lead1 + got[0, :, BLOCK : 2 * BLOCK]
        narrow = jnp.concatenate([got[group * q, :, 2 * BLOCK :] for q in range(NKIDS)], 1)
        lead2 = got[1, :, BLOCK : 2 * BLOCK] + dot3(
            narrow, jnp.concatenate([hot(q, 2) for q in range(NKIDS)], 0)
        )
        own_slice = jnp.concatenate([lead0, lead1, lead2], 1)

    with jax.named_scope("lead"):
        piece = own_slice.shape[0] // nc
        pieces = lax.all_to_all(own_slice.reshape(nc, piece, LEAD), "col", 0, 0, tiled=True)
        a00 = spread(pieces[0, :, :BLOCK], ("row", "col"), nr * nc).reshape(BLOCK, BLOCK)
        rest = jnp.concatenate([pieces[1, :, : 2 * BLOCK], pieces[2]], 1)
        rest = spread(rest, "row", nr)
        rest = lax.all_gather(rest, "col", axis=0, tiled=False)
        rest = rest.transpose(1, 0, 2, 3).reshape(BLOCK, 5 * BLOCK)

    with jax.named_scope("panel_rows"):
        perm = []
        for i in range(nr):
            for j in range(nc):
                front = j * cols_loc + i * (cols_loc // nr)
                perm.append((i * nc + j, front // rows_loc * nc + front % rows_loc // (rows_loc // nc)))
        other = lax.ppermute(own_slice, ("row", "col"), perm)
        row_rows = lax.all_gather(other, "col", axis=0, tiled=True)
        col_rows = spread(own_slice, "row", nr).reshape(cols_loc, LEAD)

    with jax.named_scope("factor"):
        l00, w0 = factor_call(factor0, 2, a00)
        l11, w1, l10 = factor_call(factor1, 3, rest[:, : 2 * BLOCK], w0)
        l22, w2, l20, l21 = factor_call(factor2, 4, rest[:, 2 * BLOCK :], w0, w1, l10)

    with jax.named_scope("extend_add"):
        arrived = lax.all_to_all(contrib.reshape(nr, PICK, PICK), "row", 0, 0, tiled=True)
        halves = []
        for h in range(group):
            rng = group * r + h
            wide = jnp.concatenate(
                [dot3(arrived[group * q + h], hot(q, c)) for q in range(NKIDS)], 0
            )
            picks = jnp.concatenate([hot(q, rng) for q in range(NKIDS)], 0)
            halves.append(dot3(picks.T, wide))
        assembled = root_front + jnp.concatenate(halves, 0)

    with jax.named_scope("solve"):
        both = jnp.concatenate([row_rows, col_rows], 0)
        s0 = dot3(both[:, :BLOCK], w0, True)
        s1 = dot3(both[:, BLOCK : 2 * BLOCK] - dot3(s0, l10, True), w1, True)
        s2 = dot3(both[:, 2 * BLOCK :] - dot3(s0, l20, True) - dot3(s1, l21, True), w2, True)
        solved = jnp.concatenate([s0, s1, s2], 1)

    with jax.named_scope("schur"):
        schur = assembled - dot3(solved[:rows_loc], solved[rows_loc:], True)
        panel = jnp.where(c == 0, s0, jnp.where(c == 1, s1, s2))[:rows_loc]
        diag = jnp.where(c == 0, l00, jnp.where(c == 1, l11, l22))
        rng = group * r + jnp.arange(rows_loc)[:, None] // BLOCK
        lead = jnp.where(rng > c, panel, jnp.where(rng == c, jnp.concatenate([diag] * group, 0), 0.0))
        return jnp.where(c < PANELS, lead, jnp.where(rng < PANELS, 0.0, schur))


def solution(mesh):
    placed = (P("row", "col"), P("row", "col"), P())
    return jax.shard_map(
        body, mesh=mesh, in_specs=placed, out_specs=P("row", "col"), check_vma=False
    )
```

```python
import jax
import jax.numpy as jnp
import numpy as np
from jax import lax
from jax.experimental import pallas as pl
from jax.experimental.pallas import tpu as pltpu
from jax.sharding import Mesh, PartitionSpec as P

CB = 4096
NKIDS = 4
BLOCK = 512
PANELS = 3
PICK = 256
LEAD = BLOCK * PANELS
F32 = jnp.float32
B16 = jnp.bfloat16


def split3(x):
    high = x.astype(B16).astype(F32)
    rest = x - high
    mid = rest.astype(B16).astype(F32)
    return high, mid, rest - mid


def outer_update(lhs, rhs):
    a_high, a_mid, a_low = split3(lhs)
    b_high, b_mid, b_low = split3(rhs)
    a = jnp.concatenate([a_high, a_high, a_mid, a_high, a_low, a_mid], 0).astype(B16)
    b = jnp.concatenate([b_high, b_mid, b_high, b_low, b_high, b_mid], 0).astype(B16)
    return lax.dot_general(a, b, (((0,), (0,)), ((), ())), preferred_element_type=F32)


def factor_tile(rows):
    count = len(rows)
    lane = lax.broadcasted_iota(jnp.int32, (8, 128), 1)
    sub = lax.broadcasted_iota(jnp.int32, (8, 128), 0)
    rows = list(rows)
    uppers, inverses = [], []
    for k in range(count):
        c0 = 8 * k
        own = (lane >= c0) & (lane < c0 + 8)
        cur = rows[k]
        nxt = rows[k + 1] if k + 1 < count else None
        top = [jnp.broadcast_to(cur[:, c0 + j : c0 + j + 1], (8, 128)) for j in range(8)]
        if nxt is not None:
            low = [jnp.broadcast_to(nxt[:, c0 + j : c0 + j + 1], (8, 128)) for j in range(8)]
            after = jnp.where(own, 0.0, nxt)
        upper = cur
        inv = jnp.where(own, jnp.where(lane - c0 == sub, 1.0, 0.0), cur)
        for j in range(8):
            scale = lax.rsqrt(jnp.broadcast_to(top[j][j : j + 1, :], (8, 128)))
            mult = jnp.where(sub > j, top[j] * scale, 0.0)
            if nxt is not None:
                low_mult = low[j] * scale
            for m in range(j + 1, 8):
                u = jnp.broadcast_to(top[m][j : j + 1, :], (8, 128)) * scale
                top[m] = top[m] - mult * u
                if nxt is not None:
                    low[m] = low[m] - low_mult * u
            u = jnp.broadcast_to(upper[j : j + 1, :], (8, 128)) * scale
            upper = jnp.where(sub == j, u, upper - mult * u)
            u = jnp.broadcast_to(inv[j : j + 1, :], (8, 128)) * scale
            inv = jnp.where(sub == j, u, inv - mult * u)
            if nxt is not None:
                after = after - low_mult * u
        uppers.append(jnp.where(lane - c0 >= sub, upper, 0.0))
        inverses.append(jnp.where(lane < c0 + 8, inv, 0.0))
        if nxt is not None:
            rows[k + 1] = after
        if k + 2 < count:
            update = outer_update(jnp.where(lane >= c0 + 16, upper, 0.0), inv)
            for i in range(k + 2, count):
                rows[i] = jnp.where(own, 0.0, rows[i]) - update[8 * i : 8 * i + 8, :]
    return uppers, inverses


def mm(a, b, flip=False):
    dims = (((1,), (1 if flip else 0,)), ((), ()))
    return lax.dot_general(a, b, dims, precision=lax.Precision.HIGHEST, preferred_element_type=F32)


def nt(a, b):
    return lax.dot_general(a, b, (((1,), (1,)), ((), ())), preferred_element_type=F32)


def split2(x):
    high = x.astype(B16)
    return high, (x - high.astype(F32)).astype(B16)


def left3(x):
    high, low = split2(x)
    return jnp.concatenate([high, high, low], 1)


def right3(x):
    high, low = split2(x)
    return jnp.concatenate([high, low, high], 1)


def mm3(a, b):
    return nt(left3(a), right3(b))


def whole(x):
    high, mid, low = split3(x)
    return jnp.concatenate([high, mid, low], 1).astype(B16)


def factor_block(l_ref, w_ref, s_ref):
    size = s_ref.shape[0]
    tiles = size // 128
    l_ref[...] = jnp.zeros_like(l_ref)
    w_ref[...] = jnp.zeros_like(w_ref)
    for k in range(tiles):
        o = 128 * k
        e = o + 128
        rows = [s_ref[o + 8 * i : o + 8 * i + 8, o:e] for i in range(16)]
        uppers, inverses = factor_tile(rows)
        inv = jnp.concatenate(inverses, 0)
        l_ref[o:e, o:e] = jnp.concatenate(uppers, 0).T
        w_ref[o:e, o:e] = inv
        if k + 1 < tiles:
            below = mm(s_ref[e:, o:e], inv, True)
            l_ref[e:, o:e] = below
            s_ref[e:, e:] = s_ref[e:, e:] - mm(below, below, True)
    half = 128
    while half < size:
        for o in range(0, size, 2 * half):
            m = o + half
            e = m + half
            t = mm(l_ref[m:e, o:m], w_ref[o:m, o:m])
            w_ref[m:e, o:m] = -mm(w_ref[m:e, m:e], t)
        half *= 2


def put_rows(dst, a_ref, b_ref, second, col):
    for q in range(8):
        for i in range(8):
            src = slice(64 * q + 8 * i, 64 * q + 8 * i + 8)
            cols = slice(col, col + BLOCK)
            dst[64 * i + 8 * q : 64 * i + 8 * q + 8, :] = jnp.where(second, b_ref[src, cols], a_ref[src, cols])


def factor0(odd_ref, mine_ref, other_ref, l_ref, w_ref, s_ref):
    put_rows(s_ref, mine_ref, other_ref, odd_ref[0] == 1, 0)
    factor_block(l_ref, w_ref, s_ref)


def factor1(odd_ref, mine_ref, other_ref, w0_ref, l_ref, w_ref, l10_ref, s_ref, x_ref):
    even = odd_ref[0] == 0
    put_rows(x_ref, mine_ref, other_ref, even, BLOCK)
    put_rows(s_ref, mine_ref, other_ref, even, 0)
    l10 = mm3(x_ref[...], w0_ref[...])
    l10_ref[...] = l10
    s_ref[...] = s_ref[...] - mm3(l10, l10)
    factor_block(l_ref, w_ref, s_ref)


def factor2(
    odd_ref, mine_ref, other_ref, w0_ref, w1_ref, l10_ref,
    l_ref, w_ref, l20_ref, l21_ref, s_ref, x_ref, y_ref,
):
    odd = odd_ref[0] == 1
    put_rows(x_ref, mine_ref, other_ref, odd, BLOCK)
    put_rows(y_ref, mine_ref, other_ref, jnp.logical_not(odd), 2 * BLOCK)
    put_rows(s_ref, mine_ref, other_ref, odd, 2 * BLOCK)
    l20 = mm3(x_ref[...].T, w0_ref[...])
    l20_ref[...] = l20
    l21 = mm3(y_ref[...].T - mm3(l20, l10_ref[...]), w1_ref[...])
    l21_ref[...] = l21
    both = jnp.concatenate([l20, l21], 1)
    s_ref[...] = s_ref[...] - mm3(both, both)
    factor_block(l_ref, w_ref, s_ref)


VMEM = pl.BlockSpec(memory_space=pltpu.VMEM)
SMEM = pl.BlockSpec(memory_space=pltpu.SMEM)
PARAMS = pltpu.CompilerParams(vmem_limit_bytes=60 << 20)


def factor_call(kernel, outs, scratch, *args):
    square = jax.ShapeDtypeStruct((BLOCK, BLOCK), F32)
    return pl.pallas_call(
        kernel,
        grid=(1,),
        in_specs=[SMEM] + [pl.BlockSpec(x.shape, lambda i: (0, 0)) for x in args[1:]],
        out_specs=[pl.BlockSpec((BLOCK, BLOCK), lambda i: (0, 0))] * outs,
        out_shape=[square] * outs,
        scratch_shapes=[pltpu.VMEM((BLOCK, BLOCK), F32)] * scratch,
        compiler_params=PARAMS,
        cost_estimate=pl.CostEstimate(flops=20_000_000_000, bytes_accessed=1 << 24, transcendentals=0),
    )(*args)


def hot_t(index, size=BLOCK):
    place = lax.broadcasted_iota(jnp.int32, (size, index.shape[1]), 0)
    return (place == index).astype(F32).astype(B16)


def three(x):
    return jnp.concatenate([x, x, x], 1)


def prepare(flag_ref, cols_ref, rows_ref, contrib_ref, root_ref, out_ref):
    cols = three(hot_t(cols_ref[...]))
    rows = three(hot_t(rows_ref[...]))
    first = nt(whole(nt(cols, whole(contrib_ref[:PICK, :]))), rows)
    third = nt(cols, whole(contrib_ref[PICK:, :]))
    root_a = root_ref[:BLOCK, :].T
    root_b = root_ref[BLOCK:, :].T
    is_first = flag_ref[0] == 0
    out_ref[:, :BLOCK] = first + jnp.where(is_first, root_a, 0.0)
    out_ref[:, BLOCK : 2 * BLOCK] = jnp.where(is_first, root_b, root_a)
    out_ref[:, 2 * BLOCK :] = third


def combine(index_ref, got_ref, out_ref):
    out_ref[:, :BLOCK] = (
        got_ref[0, :, :BLOCK] + got_ref[2, :, :BLOCK] + got_ref[4, :, :BLOCK] + got_ref[6, :, :BLOCK]
    )
    out_ref[:, BLOCK : 2 * BLOCK] = (
        got_ref[1, :, :BLOCK] + got_ref[3, :, :BLOCK] + got_ref[5, :, :BLOCK] + got_ref[7, :, :BLOCK]
        + got_ref[0, :, BLOCK : 2 * BLOCK]
    )
    total = got_ref[1, :, BLOCK : 2 * BLOCK]
    for q in range(NKIDS):
        rows = three(hot_t(index_ref[q : q + 1, :]))
        total = total + nt(whole(got_ref[2 * q, :, 2 * BLOCK :]), rows)
    out_ref[:, 2 * BLOCK :] = total


def extend_add(rows_ref, cols_ref, arrived_ref, root_ref, out_ref, wide_ref):
    for h in range(2):
        total = root_ref[h * BLOCK : (h + 1) * BLOCK, :]
        for q in range(NKIDS):
            cols = three(hot_t(cols_ref[q : q + 1, :]))
            rows = three(hot_t(rows_ref[h, q : q + 1, :]))
            wide = nt(cols, whole(arrived_ref[2 * q + h]))
            wide_ref[q] = nt(rows, whole(wide))
        out_ref[h * BLOCK : (h + 1) * BLOCK, :] = (
            total + ((wide_ref[0] + wide_ref[1]) + (wide_ref[2] + wide_ref[3]))
        )


STEP = 256


def finish(
    place_ref, cols_ref, rows_ref, front_ref, w0_ref, w1_ref, w2_ref, l10_ref, l20_ref, l21_ref,
    d0_ref, d1_ref, d2_ref, out_ref, w3_ref, m10_ref, m2_ref, c3_ref, x_ref, s_ref, raw_ref, sem,
):
    step = pl.program_id(0)
    r = place_ref[0]
    c = place_ref[1]
    sources = (w0_ref, l10_ref, w1_ref, l20_ref, l21_ref, w2_ref)
    copies = [
        pltpu.make_async_copy(src, raw_ref.at[n], sem.at[n]) for n, src in enumerate(sources)
    ]

    @pl.when(step == 0)
    def _():
        for copy in copies:
            copy.start()

    @pl.when(step < 2)
    def _():
        x_ref[...] = cols_ref[...].reshape(STEP, LEAD)

    @pl.when(step >= 2)
    def _():
        turn = 2 * ((step - 2) // 2) + lax.rem(r, 2)
        for z in range(4):
            x_ref[z * STEP // 4 : (z + 1) * STEP // 4, :] = rows_ref[lax.rem(z + turn, 4), 0, 0]

    @pl.when(step == 0)
    def _():
        copies[0].wait()
        w3_ref[0] = right3(raw_ref[0])

    s_ref[:, :BLOCK] = nt(left3(x_ref[:, :BLOCK]), w3_ref[0])

    @pl.when(step == 0)
    def _():
        copies[1].wait()
        m10_ref[...] = right3(raw_ref[1])
        copies[2].wait()
        w3_ref[1] = right3(raw_ref[2])

    s1 = nt(left3(x_ref[:, BLOCK : 2 * BLOCK] - nt(left3(s_ref[:, :BLOCK]), m10_ref[...])), w3_ref[1])
    s_ref[:, BLOCK : 2 * BLOCK] = s1

    @pl.when(step == 0)
    def _():
        copies[3].wait()
        copies[4].wait()
        m2_ref[...] = right3(jnp.concatenate([raw_ref[3], raw_ref[4]], 1))
        copies[5].wait()
        w3_ref[2] = right3(raw_ref[5])

    s2 = nt(left3(x_ref[:, 2 * BLOCK :] - nt(left3(s_ref[:, : 2 * BLOCK]), m2_ref[...])), w3_ref[2])
    s_ref[:, 2 * BLOCK :] = s2

    @pl.when(step < 2)
    def _():
        c3_ref[pl.ds(pl.multiple_of(step * STEP, STEP), STEP), :] = right3(s_ref[...])

    rng = 2 * r + (step - 2) // 2
    half = pl.ds(pl.multiple_of(lax.rem(step, 2) * STEP, STEP), STEP)

    @pl.when((step >= 2) & (c >= PANELS) & (rng >= PANELS))
    def _():
        out_ref[...] = front_ref[...] - nt(left3(s_ref[...]), c3_ref[...])

    @pl.when((step >= 2) & (rng < jnp.minimum(c, PANELS)))
    def _():
        out_ref[...] = jnp.zeros_like(out_ref)

    for p, d_ref in enumerate((d0_ref, d1_ref, d2_ref)):
        @pl.when((step >= 2) & (c == p) & (rng > p))
        def _():
            out_ref[...] = s_ref[:, p * BLOCK : (p + 1) * BLOCK]

        @pl.when((step >= 2) & (c == p) & (rng == p))
        def _():
            pltpu.sync_copy(d_ref.at[half, :], out_ref)


def finish_call(place, col_rows, row_rows, front, mats):
    blocks = lambda i: (jnp.maximum(i - 2, 0), 0)
    return pl.pallas_call(
        finish,
        grid=(6,),
        in_specs=[
            SMEM,
            pl.BlockSpec((4, 1, STEP // 4, LEAD), lambda i: (0, jnp.minimum(i, 1), 0, 0)),
            pl.BlockSpec(
                (4, 1, 1, STEP // 4, LEAD),
                lambda i: (0, jnp.maximum(i - 2, 0) % 2, jnp.maximum(i - 2, 0) // 2, 0, 0),
            ),
            pl.BlockSpec((STEP, BLOCK), blocks),
        ]
        + [pl.BlockSpec(memory_space=pl.ANY)] * 9,
        out_specs=pl.BlockSpec((STEP, BLOCK), blocks),
        out_shape=jax.ShapeDtypeStruct(front.shape, F32),
        scratch_shapes=[
            pltpu.VMEM((3, BLOCK, 3 * BLOCK), B16),
            pltpu.VMEM((BLOCK, 3 * BLOCK), B16),
            pltpu.VMEM((BLOCK, 6 * BLOCK), B16),
            pltpu.VMEM((BLOCK, 9 * BLOCK), B16),
            pltpu.VMEM((STEP, LEAD), F32),
            pltpu.VMEM((STEP, LEAD), F32),
            pltpu.VMEM((6, BLOCK, BLOCK), F32),
            pltpu.SemaphoreType.DMA((6,)),
        ],
        compiler_params=PARAMS,
        cost_estimate=pl.CostEstimate(flops=20_000_000_000, bytes_accessed=24 << 20, transcendentals=0),
    )(place, col_rows, row_rows, front, *mats)


ROW = ("x_hi", "z")
CHIP = ("y", "x_lo")
SHAPE = (2, 4, 4, 2, 2)
COL = CHIP + ("core",)


def spread(a, axis, count):
    return lax.all_to_all(jnp.broadcast_to(a[None], (count,) + a.shape), axis, 0, 0, tiled=True)


def body(root_front, contrib, index_map):
    nr = lax.axis_size(ROW)
    nc = lax.axis_size(COL)
    r = lax.axis_index(ROW)
    c = lax.axis_index(COL)
    rows_loc, cols_loc = root_front.shape
    group = nr // NKIDS
    kid = r // group
    part = r % group
    per = cols_loc // nr
    index = index_map.reshape(NKIDS, -1, PICK) - jnp.arange(CB // PICK, dtype=jnp.int32)[:, None] * BLOCK
    odd = lax.axis_index("core").reshape(1)

    def pick(kid_id, rng):
        return lax.dynamic_slice(index, (kid_id, rng, 0), (1, 1, PICK)).reshape(1, PICK)

    def gather(rows):
        mine = spread(rows, CHIP, nc // 2).reshape(-1, rows.shape[1])
        return mine, lax.ppermute(mine, "core", [(0, 1), (1, 0)])

    with jax.named_scope("slices"):
        outgoing = pl.pallas_call(
            prepare,
            grid=(1,),
            in_specs=[
                SMEM,
                VMEM,
                VMEM,
                pl.BlockSpec((2 * PICK, PICK), lambda i: (0, 0)),
                VMEM,
            ],
            out_specs=VMEM,
            out_shape=jax.ShapeDtypeStruct((cols_loc, 2 * BLOCK + PICK), F32),
            compiler_params=PARAMS,
        )(r.reshape(1), pick(kid, c), pick(kid, part), contrib, root_front)
        got = lax.all_to_all(outgoing.reshape(nr, per, -1), ROW, 0, 0, tiled=True)
        own_slice = pl.pallas_call(
            combine,
            in_specs=[VMEM, VMEM],
            out_specs=VMEM,
            out_shape=jax.ShapeDtypeStruct((per, LEAD), F32),
            compiler_params=PARAMS,
        )(index[:, 2, :], got)

    with jax.named_scope("panel_cols"):
        far = lax.ppermute(own_slice, "x_hi", [(0, 1), (1, 0)])

    with jax.named_scope("lead"):
        pieces = lax.all_to_all(own_slice.reshape(nc // 2, per // (nc // 2), LEAD), CHIP, 0, 0, tiled=True)
        pieces, far, early = lax.optimization_barrier((pieces, far, own_slice))
        top, last = pieces[0], pieces[1]
        even_blocks = [top[:, :BLOCK], top[:, 2 * BLOCK :], last[:, 2 * BLOCK :]]
        odd_blocks = [top[:, BLOCK : 2 * BLOCK], top[:, :BLOCK], top[:, 2 * BLOCK :]]
        strip = jnp.where(odd[0] == 1, jnp.concatenate(odd_blocks, 1), jnp.concatenate(even_blocks, 1))
        strip = spread(strip, ROW, nr).reshape(-1, LEAD)
        mine, other = gather(strip)
        mine, other, own_slice = lax.optimization_barrier((mine, other, own_slice))

    with jax.named_scope("panel_cols"):
        high = lax.axis_index("x_hi") == 1
        pair = jnp.stack([jnp.where(high, far, early), jnp.where(high, early, far)])
        col_rows = lax.all_gather(pair, "z", axis=0, tiled=False)

    with jax.named_scope("panel_rows"):
        perm = []
        for n in range(nr * nc):
            x_hi, z, y, x_lo, core = (int(v) for v in np.unravel_index(n, SHAPE))
            row = y * 2 + x_lo
            to = (row // 4, row % 4, (z + 2 * core + x_lo) % 4, x_hi, core)
            perm.append((n, int(np.ravel_multi_index(to, SHAPE))))
        share = lax.ppermute(own_slice, ROW + COL, perm)

    with jax.named_scope("factor"):
        l00, w0 = factor_call(factor0, 2, 1, odd, mine, other)

    with jax.named_scope("panel_rows"):
        w0, contrib, share = lax.optimization_barrier((w0, contrib, share))
        row_rows = lax.all_gather(share, COL, axis=0, tiled=False)
        row_rows = row_rows.reshape(4, 2, 2, per, LEAD)

    with jax.named_scope("exchange"):
        arrived = lax.all_to_all(contrib.reshape(nr, PICK, PICK), ROW, 0, 0, tiled=True)

    with jax.named_scope("factor"):
        l11, w1, l10 = factor_call(factor1, 3, 2, odd, mine, other, w0)
        l22, w2, l20, l21 = factor_call(factor2, 4, 3, odd, mine, other, w0, w1, l10)

    with jax.named_scope("extend_add"):
        w2, arrived = lax.optimization_barrier((w2, arrived))
        own_rows = lax.dynamic_slice(index, (0, group * r, 0), (NKIDS, group, PICK)).transpose(1, 0, 2)
        own_cols = lax.dynamic_slice(index, (0, c, 0), (NKIDS, 1, PICK)).reshape(NKIDS, PICK)
        front = pl.pallas_call(
            extend_add,
            in_specs=[VMEM] * 4,
            out_specs=VMEM,
            out_shape=jax.ShapeDtypeStruct(root_front.shape, F32),
            scratch_shapes=[pltpu.VMEM((NKIDS, BLOCK, BLOCK), F32)],
            compiler_params=PARAMS,
            cost_estimate=pl.CostEstimate(flops=5_000_000_000, bytes_accessed=6 << 20, transcendentals=0),
        )(own_rows, own_cols, arrived, root_front)

    with jax.named_scope("finish"):
        place = jnp.stack([r, c])
        return finish_call(
            place, col_rows, row_rows, front, (w0, w1, w2, l10, l20, l21, l00, l11, l22)
        )


def solution(mesh):
    torus = Mesh(mesh.devices.reshape(SHAPE), ROW + COL)
    placed = (P(ROW, COL), P(ROW, COL), P())
    return jax.shard_map(
        body, mesh=torus, in_specs=placed, out_specs=P(ROW, COL), check_vma=False
    )
```

```python
import jax
import jax.numpy as jnp
from jax import lax
from jax.experimental import pallas as pl
from jax.experimental.pallas import tpu as pltpu
from jax.sharding import Mesh, PartitionSpec as P

CB = 4096
NKIDS = 4
BLOCK = 512
PANELS = 3
PICK = 256
LEAD = BLOCK * PANELS
F32 = jnp.float32
B16 = jnp.bfloat16


def split3(x):
    high = x.astype(B16).astype(F32)
    rest = x - high
    mid = rest.astype(B16).astype(F32)
    return high, mid, rest - mid


def outer_update(lhs, rhs):
    a_high, a_mid, a_low = split3(lhs)
    b_high, b_mid, b_low = split3(rhs)
    a = jnp.concatenate([a_high, a_high, a_mid, a_high, a_low, a_mid], 0).astype(B16)
    b = jnp.concatenate([b_high, b_mid, b_high, b_low, b_high, b_mid], 0).astype(B16)
    return lax.dot_general(a, b, (((0,), (0,)), ((), ())), preferred_element_type=F32)


def factor_tile(rows):
    count = len(rows)
    lane = lax.broadcasted_iota(jnp.int32, (8, 128), 1)
    sub = lax.broadcasted_iota(jnp.int32, (8, 128), 0)
    wide = lambda x: jnp.broadcast_to(x, (8, 128))
    rows = list(rows)
    uppers, inverses = [], []
    for k in range(count):
        c0 = 8 * k
        own = (lane >= c0) & (lane < c0 + 8)
        cur = rows[k]
        top = [wide(cur[:, c0 + j : c0 + j + 1]) for j in range(8)]
        near = range(k + 1, min(k + 3, count))
        lows = [[wide(rows[n][:, c0 + j : c0 + j + 1]) for j in range(8)] for n in near]
        afters = [jnp.where(own, 0.0, rows[n]) for n in near]
        upper = cur
        inv = jnp.where(own, jnp.where(lane - c0 == sub, 1.0, 0.0), cur)
        for j in range(8):
            scale = lax.rsqrt(wide(top[j][j : j + 1, :]))
            mult = jnp.where(sub > j, top[j] * scale, 0.0)
            low_mults = [low[j] * scale for low in lows]
            for m in range(j + 1, 8):
                u = wide(top[m][j : j + 1, :]) * scale
                top[m] = top[m] - mult * u
                for low, low_mult in zip(lows, low_mults):
                    low[m] = low[m] - low_mult * u
            u = wide(upper[j : j + 1, :]) * scale
            upper = jnp.where(sub == j, u, upper - mult * u)
            u = wide(inv[j : j + 1, :]) * scale
            inv = jnp.where(sub == j, u, inv - mult * u)
            afters = [after - low_mult * u for after, low_mult in zip(afters, low_mults)]
        uppers.append(jnp.where(lane - c0 >= sub, upper, 0.0))
        inverses.append(jnp.where(lane < c0 + 8, inv, 0.0))
        for n, after in zip(near, afters):
            rows[n] = after
        if k + 3 < count:
            update = outer_update(jnp.where(lane >= c0 + 24, upper, 0.0), inv)
            for i in range(k + 3, count):
                rows[i] = jnp.where(own, 0.0, rows[i]) - update[8 * i : 8 * i + 8, :]
    return uppers, inverses


def mm(a, b, flip=False):
    dims = (((1,), (1 if flip else 0,)), ((), ()))
    return lax.dot_general(a, b, dims, precision=lax.Precision.HIGHEST, preferred_element_type=F32)


def nt(a, b):
    return lax.dot_general(a, b, (((1,), (1,)), ((), ())), preferred_element_type=F32)


def split2(x):
    high = x.astype(B16)
    return high, (x - high.astype(F32)).astype(B16)


def left3(x):
    high, low = split2(x)
    return jnp.concatenate([high, high, low], 1)


def right3(x):
    high, low = split2(x)
    return jnp.concatenate([high, low, high], 1)


def mm3(a, b):
    return nt(left3(a), right3(b))


def whole(x):
    high, mid, low = split3(x)
    return jnp.concatenate([high, mid, low], 1).astype(B16)


def factor_block(l_ref, w_ref, s_ref):
    size = s_ref.shape[0]
    tiles = size // 128
    l_ref[...] = jnp.zeros_like(l_ref)
    w_ref[...] = jnp.zeros_like(w_ref)
    for k in range(tiles):
        o = 128 * k
        e = o + 128
        rows = [s_ref[o + 8 * i : o + 8 * i + 8, o:e] for i in range(16)]
        uppers, inverses = factor_tile(rows)
        inv = jnp.concatenate(inverses, 0)
        l_ref[o:e, o:e] = jnp.concatenate(uppers, 0).T
        w_ref[o:e, o:e] = inv
        if k + 1 < tiles:
            below = mm(s_ref[e:, o:e], inv, True)
            l_ref[e:, o:e] = below
            s_ref[e:, e:] = s_ref[e:, e:] - mm(below, below, True)
    half = 128
    while half < size:
        for o in range(0, size, 2 * half):
            m = o + half
            e = m + half
            t = mm(l_ref[m:e, o:m], w_ref[o:m, o:m])
            w_ref[m:e, o:m] = -mm(w_ref[m:e, m:e], t)
        half *= 2


def put_rows(dst, a_ref, b_ref, second, col):
    for q in range(8):
        for i in range(8):
            src = slice(64 * q + 8 * i, 64 * q + 8 * i + 8)
            cols = slice(col, col + BLOCK)
            dst[64 * i + 8 * q : 64 * i + 8 * q + 8, :] = jnp.where(second, b_ref[src, cols], a_ref[src, cols])


def factor0(odd_ref, mine_ref, other_ref, l_ref, w_ref, s_ref):
    put_rows(s_ref, mine_ref, other_ref, odd_ref[0] == 1, 0)
    factor_block(l_ref, w_ref, s_ref)


def factor1(odd_ref, mine1_ref, other1_ref, mine2_ref, other2_ref, w0_ref, l_ref, w_ref, l10_ref, s_ref, x_ref):
    even = odd_ref[0] == 0
    put_rows(x_ref, mine2_ref, other2_ref, even, 0)
    put_rows(s_ref, mine1_ref, other1_ref, even, 0)
    l10 = mm3(x_ref[...], w0_ref[...])
    l10_ref[...] = l10
    s_ref[...] = s_ref[...] - mm3(l10, l10)
    factor_block(l_ref, w_ref, s_ref)


def factor2(
    odd_ref, mine_ref, other_ref, w0_ref, w1_ref, l10_ref,
    l_ref, w_ref, l20_ref, l21_ref, s_ref, x_ref, y_ref,
):
    odd = odd_ref[0] == 1
    put_rows(x_ref, mine_ref, other_ref, odd, 0)
    put_rows(y_ref, mine_ref, other_ref, jnp.logical_not(odd), BLOCK)
    put_rows(s_ref, mine_ref, other_ref, odd, BLOCK)
    l20 = mm3(x_ref[...].T, w0_ref[...])
    l20_ref[...] = l20
    l21 = mm3(y_ref[...].T - mm3(l20, l10_ref[...]), w1_ref[...])
    l21_ref[...] = l21
    both = jnp.concatenate([l20, l21], 1)
    s_ref[...] = s_ref[...] - mm3(both, both)
    factor_block(l_ref, w_ref, s_ref)


VMEM = pl.BlockSpec(memory_space=pltpu.VMEM)
SMEM = pl.BlockSpec(memory_space=pltpu.SMEM)
PARAMS = pltpu.CompilerParams(vmem_limit_bytes=60 << 20)


def factor_call(kernel, outs, scratch, *args):
    square = jax.ShapeDtypeStruct((BLOCK, BLOCK), F32)
    return pl.pallas_call(
        kernel,
        grid=(1,),
        in_specs=[SMEM] + [pl.BlockSpec(x.shape, lambda i: (0, 0)) for x in args[1:]],
        out_specs=[pl.BlockSpec((BLOCK, BLOCK), lambda i: (0, 0))] * outs,
        out_shape=[square] * outs,
        scratch_shapes=[pltpu.VMEM((BLOCK, BLOCK), F32)] * scratch,
        compiler_params=PARAMS,
        cost_estimate=pl.CostEstimate(flops=20_000_000_000, bytes_accessed=1 << 24, transcendentals=0),
    )(*args)


def hot_t(index, size=BLOCK):
    place = lax.broadcasted_iota(jnp.int32, (size, index.shape[1]), 0)
    return (place == index).astype(F32).astype(B16)


def three(x):
    return jnp.concatenate([x, x, x], 1)


def prepare(flag_ref, cols_ref, rows_ref, contrib_ref, root_ref, out_ref):
    cols = three(hot_t(cols_ref[...]))
    rows = three(hot_t(rows_ref[...]))
    first = nt(whole(nt(cols, whole(contrib_ref[:PICK, :]))), rows)
    third = nt(cols, whole(contrib_ref[PICK:, :]))
    root_a = root_ref[:BLOCK, :].T
    root_b = root_ref[BLOCK:, :].T
    is_first = flag_ref[0] == 0
    out_ref[:, :BLOCK] = first + jnp.where(is_first, root_a, 0.0)
    out_ref[:, BLOCK : 2 * BLOCK] = jnp.where(is_first, root_b, root_a)
    out_ref[:, 2 * BLOCK :] = third


def combine(index_ref, first_ref, second_ref, third_ref, out_ref):
    out_ref[:, :BLOCK] = (first_ref[0] + first_ref[2]) + (first_ref[4] + first_ref[6])
    out_ref[:, BLOCK : 2 * BLOCK] = (
        (first_ref[1] + first_ref[3]) + (first_ref[5] + first_ref[7]) + second_ref[0]
    )
    total = second_ref[1]
    for q in range(NKIDS):
        total = total + nt(whole(third_ref[2 * q]), three(hot_t(index_ref[q : q + 1, :])))
    out_ref[:, 2 * BLOCK :] = total


def two(x):
    return jnp.concatenate([x, x], 1)


def finish(
    place_ref, cols_ref, rows_ref, front_ref, arrived_ref, row_hot_ref, col_hot_ref, w0_ref, w1_ref, w2_ref, l10_ref, l20_ref, l21_ref,
    d0_ref, d1_ref, d2_ref, out_ref, w3_ref, m10_ref, m2_ref, c3_ref, x_ref, s_ref, raw_ref, sem,
):
    step = pl.program_id(0)
    r = place_ref[0]
    c = place_ref[1]
    part = x_ref.shape[0] // 8
    sources = (w0_ref, l10_ref, w1_ref, l20_ref, l21_ref, w2_ref)
    copies = [
        pltpu.make_async_copy(src, raw_ref.at[n], sem.at[n]) for n, src in enumerate(sources)
    ]

    @pl.when(step == 0)
    def _():
        for copy in copies:
            copy.start()
        for n in range(8):
            x_ref[n * part : (n + 1) * part, :] = cols_ref[n % 4, n // 4]

    @pl.when(step > 0)
    def _():
        for q in range(8):
            for n in range(8):
                to = n * part + 8 * q
                x_ref[to : to + 8, :] = rows_ref[q, 0, 8 * n : 8 * n + 8, :]

    @pl.when(step == 0)
    def _():
        copies[0].wait()
        w3_ref[0] = right3(raw_ref[0])

    s_ref[:, :BLOCK] = nt(left3(x_ref[:, :BLOCK]), w3_ref[0])

    @pl.when(step == 0)
    def _():
        copies[1].wait()
        m10_ref[...] = right3(raw_ref[1])
        copies[2].wait()
        w3_ref[1] = right3(raw_ref[2])

    s1 = nt(left3(x_ref[:, BLOCK : 2 * BLOCK] - nt(left3(s_ref[:, :BLOCK]), m10_ref[...])), w3_ref[1])
    s_ref[:, BLOCK : 2 * BLOCK] = s1

    @pl.when(step == 0)
    def _():
        copies[3].wait()
        copies[4].wait()
        m2_ref[...] = right3(jnp.concatenate([raw_ref[3], raw_ref[4]], 1))
        copies[5].wait()
        w3_ref[2] = right3(raw_ref[5])

    s2 = nt(left3(x_ref[:, 2 * BLOCK :] - nt(left3(s_ref[:, : 2 * BLOCK]), m2_ref[...])), w3_ref[2])
    s_ref[:, 2 * BLOCK :] = s2

    @pl.when(step == 0)
    def _():
        c3_ref[...] = right3(s_ref[...])

    rng = 2 * r + step - 1

    @pl.when((step > 0) & (c >= PANELS) & (rng >= PANELS))
    def _():
        total = front_ref[...]
        for q in range(NKIDS):
            cols = two(hot_t(col_hot_ref[q : q + 1, :]))
            rows = two(hot_t(row_hot_ref[step - 1, q : q + 1, :]))
            spread_cols = nt(cols, jnp.concatenate(split2(arrived_ref[q, 0]), 1))
            total = total + nt(rows, jnp.concatenate(split2(spread_cols), 1))
        out_ref[...] = total - nt(left3(s_ref[...]), c3_ref[...])

    @pl.when((step > 0) & (rng < jnp.minimum(c, PANELS)))
    def _():
        out_ref[...] = jnp.zeros_like(out_ref)

    for p, d_ref in enumerate((d0_ref, d1_ref, d2_ref)):
        @pl.when((step > 0) & (c == p) & (rng > p))
        def _():
            out_ref[...] = s_ref[:, p * BLOCK : (p + 1) * BLOCK]

        @pl.when((step > 0) & (c == p) & (rng == p))
        def _():
            pltpu.sync_copy(d_ref, out_ref)


def finish_call(place, col_rows, row_rows, front, arrived, row_hot, col_hot, mats):
    half = lambda i: jnp.maximum(i - 1, 0)
    return pl.pallas_call(
        finish,
        grid=(3,),
        in_specs=[
            SMEM,
            pl.BlockSpec((4, 2, BLOCK // 8, LEAD), lambda i: (0, 0, 0, 0)),
            pl.BlockSpec((8, 1, BLOCK // 8, LEAD), lambda i: (0, half(i), 0, 0)),
            pl.BlockSpec((BLOCK, BLOCK), lambda i: (half(i), 0)),
            pl.BlockSpec((NKIDS, 1, PICK, PICK), lambda i: (0, half(i), 0, 0)),
            VMEM,
            VMEM,
        ]
        + [pl.BlockSpec(memory_space=pl.ANY)] * 9,
        out_specs=pl.BlockSpec((BLOCK, BLOCK), lambda i: (half(i), 0)),
        out_shape=jax.ShapeDtypeStruct(front.shape, F32),
        scratch_shapes=[
            pltpu.VMEM((3, BLOCK, 3 * BLOCK), B16),
            pltpu.VMEM((BLOCK, 3 * BLOCK), B16),
            pltpu.VMEM((BLOCK, 6 * BLOCK), B16),
            pltpu.VMEM((BLOCK, 9 * BLOCK), B16),
            pltpu.VMEM((BLOCK, LEAD), F32),
            pltpu.VMEM((BLOCK, LEAD), F32),
            pltpu.VMEM((6, BLOCK, BLOCK), F32),
            pltpu.SemaphoreType.DMA((6,)),
        ],
        compiler_params=PARAMS,
        cost_estimate=pl.CostEstimate(flops=20_000_000_000, bytes_accessed=24 << 20, transcendentals=0),
    )(place, col_rows, row_rows, front, arrived, row_hot, col_hot, *mats)


ROW = ("x_hi", "z")
CHIP = ("y", "x_lo")
SHAPE = (2, 4, 4, 2, 2)
COL = CHIP + ("core",)


def copies_of(a, count):
    return jnp.broadcast_to(a[None], (count,) + a.shape)


def spread(a, axis, count):
    return lax.all_to_all(copies_of(a, count), axis, 0, 0, tiled=True)


def body(root_front, contrib, index_map):
    nr = lax.axis_size(ROW)
    nc = lax.axis_size(COL)
    r = lax.axis_index(ROW)
    c = lax.axis_index(COL)
    rows_loc, cols_loc = root_front.shape
    group = nr // NKIDS
    kid = r // group
    part = r % group
    per = cols_loc // nr
    index = index_map.reshape(NKIDS, -1, PICK) - jnp.arange(CB // PICK, dtype=jnp.int32)[:, None] * BLOCK
    odd = lax.axis_index("core").reshape(1)

    def pick(kid_id, rng):
        return lax.dynamic_slice(index, (kid_id, rng, 0), (1, 1, PICK)).reshape(1, PICK)

    def swap(rows):
        return lax.ppermute(rows, "core", [(0, 1), (1, 0)])

    with jax.named_scope("slices"):
        outgoing = pl.pallas_call(
            prepare,
            grid=(1,),
            in_specs=[
                SMEM,
                VMEM,
                VMEM,
                pl.BlockSpec((2 * PICK, PICK), lambda i: (0, 0)),
                VMEM,
            ],
            out_specs=VMEM,
            out_shape=jax.ShapeDtypeStruct((cols_loc, 2 * BLOCK + PICK), F32),
            compiler_params=PARAMS,
        )(r.reshape(1), pick(kid, c), pick(kid, part), contrib, root_front)
        got = lax.all_to_all(outgoing.reshape(nr, per, -1), ROW, 0, 0, tiled=True)
        own_slice = pl.pallas_call(
            combine,
            grid=(1,),
            in_specs=[
                VMEM,
                pl.BlockSpec((nr, per, BLOCK), lambda i: (0, 0, 0)),
                pl.BlockSpec((2, per, BLOCK), lambda i: (0, 0, 1)),
                pl.BlockSpec((nr, per, PICK), lambda i: (0, 0, 2 * BLOCK // PICK)),
            ],
            out_specs=VMEM,
            out_shape=jax.ShapeDtypeStruct((per, LEAD), F32),
            compiler_params=PARAMS,
        )(index[:, 2, :], got, got, got)

    with jax.named_scope("panel_cols"):
        far = lax.ppermute(own_slice, "x_hi", [(0, 1), (1, 0)])

    with jax.named_scope("lead"):
        pieces = lax.all_to_all(own_slice.reshape(nc // 2, per // (nc // 2), LEAD), CHIP, 0, 0, tiled=True)
        pieces, far, early = lax.optimization_barrier((pieces, far, own_slice))
        top, last = pieces[0], pieces[1]
        even_blocks = [top[:, :BLOCK], top[:, 2 * BLOCK :], last[:, 2 * BLOCK :]]
        odd_blocks = [top[:, BLOCK : 2 * BLOCK], top[:, :BLOCK], top[:, 2 * BLOCK :]]
        strip = jnp.where(odd[0] == 1, jnp.concatenate(odd_blocks, 1), jnp.concatenate(even_blocks, 1))
        both = jnp.concatenate([copies_of(strip, nr), pieces], 1)
        both = lax.all_to_all(both, ROW, 0, 0, tiled=True)
        strip = both[:, : pieces.shape[1]].reshape(-1, LEAD)
        share = both[:, pieces.shape[1] :].reshape(-1, LEAD)
        mine1 = spread(strip[:, :BLOCK], CHIP, nc // 2).reshape(-1, BLOCK)
        other1 = swap(mine1)
        fan = copies_of(strip[:, BLOCK:], nc // 2)
        mine1, other1, fan = lax.optimization_barrier((mine1, other1, fan))
        mine2 = lax.all_to_all(fan, CHIP, 0, 0, tiled=True).reshape(-1, 2 * BLOCK)

    with jax.named_scope("panel_cols"):
        high = lax.axis_index("x_hi") == 1
        pair = jnp.stack([jnp.where(high, far, early), jnp.where(high, early, far)])
        col_rows = lax.all_gather(pair, "z", axis=0, tiled=False)

    with jax.named_scope("factor"):
        l00, w0 = factor_call(factor0, 2, 1, odd, mine1, other1)

    with jax.named_scope("panel_rows"):
        w0, contrib, mine2, share = lax.optimization_barrier((w0, contrib, mine2, share))
        other2 = swap(mine2)
        row_rows = lax.all_gather(share, COL, axis=0, tiled=False)
        row_rows = row_rows.reshape(nc // 2, 2, per, LEAD)

    with jax.named_scope("exchange"):
        arrived = lax.all_to_all(contrib.reshape(nr, PICK, PICK), ROW, 0, 0, tiled=True)

    with jax.named_scope("factor"):
        l11, w1, l10 = factor_call(factor1, 3, 2, odd, mine1, other1, mine2, other2, w0)
        l22, w2, l20, l21 = factor_call(factor2, 4, 3, odd, mine2, other2, w0, w1, l10)

    with jax.named_scope("finish"):
        row_hot = lax.dynamic_slice(index, (0, group * r, 0), (NKIDS, group, PICK)).transpose(1, 0, 2)
        col_hot = lax.dynamic_slice(index, (0, c, 0), (NKIDS, 1, PICK)).reshape(NKIDS, PICK)
        return finish_call(
            jnp.stack([r, c]),
            col_rows,
            row_rows,
            root_front,
            arrived.reshape(NKIDS, group, PICK, PICK),
            row_hot,
            col_hot,
            (w0, w1, w2, l10, l20, l21, l00, l11, l22),
        )


def solution(mesh):
    torus = Mesh(mesh.devices.reshape(SHAPE), ROW + COL)
    placed = (P(ROW, COL), P(ROW, COL), P())
    return jax.shard_map(
        body, mesh=torus, in_specs=placed, out_specs=P(ROW, COL), check_vma=False
    )
```

```python
import jax
import jax.numpy as jnp
from jax import lax
from jax.experimental import pallas as pl
from jax.experimental.pallas import tpu as pltpu
from jax.sharding import Mesh, PartitionSpec as P

CB = 4096
NKIDS = 4
BLOCK = 512
PANELS = 3
PICK = 256
LEAD = BLOCK * PANELS
F32 = jnp.float32
B16 = jnp.bfloat16


def split3(x):
    high = x.astype(B16).astype(F32)
    rest = x - high
    mid = rest.astype(B16).astype(F32)
    return high, mid, rest - mid


def outer_update(lhs, rhs):
    a_high, a_mid, a_low = split3(lhs)
    b_high, b_mid, b_low = split3(rhs)
    a = jnp.concatenate([a_high, a_high, a_mid, a_high, a_low, a_mid], 0).astype(B16)
    b = jnp.concatenate([b_high, b_mid, b_high, b_low, b_high, b_mid], 0).astype(B16)
    return lax.dot_general(a, b, (((0,), (0,)), ((), ())), preferred_element_type=F32)


def factor_tile(rows):
    count = len(rows)
    lane = lax.broadcasted_iota(jnp.int32, (8, 128), 1)
    sub = lax.broadcasted_iota(jnp.int32, (8, 128), 0)
    wide = lambda x: jnp.broadcast_to(x, (8, 128))
    rows = list(rows)
    uppers, inverses = [], []
    for k in range(count):
        c0 = 8 * k
        own = (lane >= c0) & (lane < c0 + 8)
        cur = rows[k]
        top = [wide(cur[:, c0 + j : c0 + j + 1]) for j in range(8)]
        near = range(k + 1, min(k + 3, count))
        lows = [[wide(rows[n][:, c0 + j : c0 + j + 1]) for j in range(8)] for n in near]
        afters = [jnp.where(own, 0.0, rows[n]) for n in near]
        upper = cur
        inv = jnp.where(own, jnp.where(lane - c0 == sub, 1.0, 0.0), cur)
        for j in range(8):
            scale = lax.rsqrt(wide(top[j][j : j + 1, :]))
            mult = jnp.where(sub > j, top[j] * scale, 0.0)
            low_mults = [low[j] * scale for low in lows]
            for m in range(j + 1, 8):
                u = wide(top[m][j : j + 1, :]) * scale
                top[m] = top[m] - mult * u
                for low, low_mult in zip(lows, low_mults):
                    low[m] = low[m] - low_mult * u
            u = wide(upper[j : j + 1, :]) * scale
            upper = jnp.where(sub == j, u, upper - mult * u)
            u = wide(inv[j : j + 1, :]) * scale
            inv = jnp.where(sub == j, u, inv - mult * u)
            afters = [after - low_mult * u for after, low_mult in zip(afters, low_mults)]
        uppers.append(jnp.where(lane - c0 >= sub, upper, 0.0))
        inverses.append(jnp.where(lane < c0 + 8, inv, 0.0))
        for n, after in zip(near, afters):
            rows[n] = after
        if k + 3 < count:
            update = outer_update(jnp.where(lane >= c0 + 24, upper, 0.0), inv)
            for i in range(k + 3, count):
                rows[i] = jnp.where(own, 0.0, rows[i]) - update[8 * i : 8 * i + 8, :]
    return uppers, inverses


def mm(a, b, flip=False):
    dims = (((1,), (1 if flip else 0,)), ((), ()))
    return lax.dot_general(a, b, dims, precision=lax.Precision.HIGHEST, preferred_element_type=F32)


def nt(a, b):
    return lax.dot_general(a, b, (((1,), (1,)), ((), ())), preferred_element_type=F32)


def split2(x):
    high = x.astype(B16)
    return high, (x - high.astype(F32)).astype(B16)


def left3(x):
    high, low = split2(x)
    return jnp.concatenate([high, high, low], 1)


def right3(x):
    high, low = split2(x)
    return jnp.concatenate([high, low, high], 1)


def mm3(a, b):
    return nt(left3(a), right3(b))


def whole(x):
    high, mid, low = split3(x)
    return jnp.concatenate([high, mid, low], 1).astype(B16)


def factor_block(l_ref, w_ref, s_ref):
    size = s_ref.shape[0]
    tiles = size // 128
    l_ref[...] = jnp.zeros_like(l_ref)
    w_ref[...] = jnp.zeros_like(w_ref)
    for k in range(tiles):
        o = 128 * k
        e = o + 128
        rows = [s_ref[o + 8 * i : o + 8 * i + 8, o:e] for i in range(16)]
        uppers, inverses = factor_tile(rows)
        inv = jnp.concatenate(inverses, 0)
        l_ref[o:e, o:e] = jnp.concatenate(uppers, 0).T
        w_ref[o:e, o:e] = inv
        if k + 1 < tiles:
            below = mm(s_ref[e:, o:e], inv, True)
            l_ref[e:, o:e] = below
            s_ref[e:, e:] = s_ref[e:, e:] - mm(below, below, True)
    half = 128
    while half < size:
        for o in range(0, size, 2 * half):
            m = o + half
            e = m + half
            t = mm(l_ref[m:e, o:m], w_ref[o:m, o:m])
            w_ref[m:e, o:m] = -mm(w_ref[m:e, m:e], t)
        half *= 2


def put_rows(dst, a_ref, b_ref, second, col):
    for q in range(8):
        for i in range(8):
            src = slice(64 * q + 8 * i, 64 * q + 8 * i + 8)
            cols = slice(col, col + BLOCK)
            dst[64 * i + 8 * q : 64 * i + 8 * q + 8, :] = jnp.where(second, b_ref[src, cols], a_ref[src, cols])


def factor0(odd_ref, mine_ref, other_ref, l_ref, w_ref, s_ref):
    put_rows(s_ref, mine_ref, other_ref, odd_ref[0] == 1, 0)
    factor_block(l_ref, w_ref, s_ref)


def factor1(odd_ref, mine1_ref, other1_ref, mine2_ref, other2_ref, w0_ref, l_ref, w_ref, l10_ref, s_ref, x_ref):
    even = odd_ref[0] == 0
    put_rows(x_ref, mine2_ref, other2_ref, even, 0)
    put_rows(s_ref, mine1_ref, other1_ref, even, 0)
    l10 = mm3(x_ref[...], w0_ref[...])
    l10_ref[...] = l10
    s_ref[...] = s_ref[...] - mm3(l10, l10)
    factor_block(l_ref, w_ref, s_ref)


def factor2(
    odd_ref, mine_ref, other_ref, w0_ref, w1_ref, l10_ref,
    l_ref, w_ref, l20_ref, l21_ref, s_ref, x_ref, y_ref,
):
    odd = odd_ref[0] == 1
    put_rows(x_ref, mine_ref, other_ref, odd, 0)
    put_rows(y_ref, mine_ref, other_ref, jnp.logical_not(odd), BLOCK)
    put_rows(s_ref, mine_ref, other_ref, odd, BLOCK)
    l20 = mm3(x_ref[...].T, w0_ref[...])
    l20_ref[...] = l20
    l21 = mm3(y_ref[...].T - mm3(l20, l10_ref[...]), w1_ref[...])
    l21_ref[...] = l21
    both = jnp.concatenate([l20, l21], 1)
    s_ref[...] = s_ref[...] - mm3(both, both)
    factor_block(l_ref, w_ref, s_ref)


VMEM = pl.BlockSpec(memory_space=pltpu.VMEM)
SMEM = pl.BlockSpec(memory_space=pltpu.SMEM)
PARAMS = pltpu.CompilerParams(vmem_limit_bytes=60 << 20)
SMALL = pltpu.CompilerParams(vmem_limit_bytes=16 << 20)
MIDDLE = pltpu.CompilerParams(vmem_limit_bytes=28 << 20)
LARGE = pltpu.CompilerParams(vmem_limit_bytes=46 << 20)


def factor_call(kernel, outs, scratch, *args):
    square = jax.ShapeDtypeStruct((BLOCK, BLOCK), F32)
    return pl.pallas_call(
        kernel,
        in_specs=[SMEM] + [VMEM] * (len(args) - 1),
        out_specs=[VMEM] * outs,
        out_shape=[square] * outs,
        scratch_shapes=[pltpu.VMEM((BLOCK, BLOCK), F32)] * scratch,
        compiler_params=MIDDLE,
        cost_estimate=pl.CostEstimate(flops=20_000_000_000, bytes_accessed=1 << 24, transcendentals=0),
    )(*args)


def hot_t(index, size=BLOCK):
    place = lax.broadcasted_iota(jnp.int32, (size, index.shape[1]), 0)
    return (place == index).astype(F32).astype(B16)


def three(x):
    return jnp.concatenate([x, x, x], 1)


def prepare(flag_ref, cols_ref, rows_ref, contrib_ref, root_ref, out_ref):
    cols = three(hot_t(cols_ref[...]))
    rows = three(hot_t(rows_ref[...]))
    first = nt(whole(nt(cols, whole(contrib_ref[:PICK, :]))), rows)
    third = nt(cols, whole(contrib_ref[PICK:, :]))
    root_a = root_ref[:BLOCK, :].T
    root_b = root_ref[BLOCK:, :].T
    is_first = flag_ref[0] == 0
    out_ref[:, :BLOCK] = first + jnp.where(is_first, root_a, 0.0)
    out_ref[:, BLOCK : 2 * BLOCK] = jnp.where(is_first, root_b, root_a)
    out_ref[:, 2 * BLOCK :] = third


def combine(index_ref, got_ref, out_ref):
    first = lambda n: got_ref[n, :, :BLOCK]
    out_ref[:, :BLOCK] = (first(0) + first(2)) + (first(4) + first(6))
    out_ref[:, BLOCK : 2 * BLOCK] = (
        (first(1) + first(3)) + (first(5) + first(7)) + got_ref[0, :, BLOCK : 2 * BLOCK]
    )
    total = got_ref[1, :, BLOCK : 2 * BLOCK]
    for q in range(NKIDS):
        rows = three(hot_t(index_ref[q : q + 1, :]))
        total = total + nt(whole(got_ref[2 * q, :, 2 * BLOCK :]), rows)
    out_ref[:, 2 * BLOCK :] = total


def two(x):
    return jnp.concatenate([x, x], 1)


def solve_cols(cols_ref, w0_ref, w1_ref, w2_ref, l10_ref, l20_ref, l21_ref, out_ref, x_ref):
    part = x_ref.shape[0] // 8
    for n in range(8):
        x_ref[n * part : (n + 1) * part, :] = cols_ref[n % 4, n // 4]
    s0 = mm3(x_ref[:, :BLOCK], w0_ref[...])
    out_ref[:, :BLOCK] = s0
    s1 = mm3(x_ref[:, BLOCK : 2 * BLOCK] - mm3(s0, l10_ref[...]), w1_ref[...])
    out_ref[:, BLOCK : 2 * BLOCK] = s1
    early = mm3(jnp.concatenate([s0, s1], 1), jnp.concatenate([l20_ref[...], l21_ref[...]], 1))
    out_ref[:, 2 * BLOCK :] = mm3(x_ref[:, 2 * BLOCK :] - early, w2_ref[...])


def solve_cols_call(col_rows, mats):
    return pl.pallas_call(
        solve_cols,
        in_specs=[VMEM] * 7,
        out_specs=VMEM,
        out_shape=jax.ShapeDtypeStruct((BLOCK, LEAD), F32),
        scratch_shapes=[pltpu.VMEM((BLOCK, LEAD), F32)],
        compiler_params=MIDDLE,
        cost_estimate=pl.CostEstimate(flops=10_000_000_000, bytes_accessed=12 << 20, transcendentals=0),
    )(col_rows, *mats)


def finish(
    place_ref, rows_ref, front_ref, arrived_ref, row_hot_ref, col_hot_ref,
    solved_ref, w0_ref, w1_ref, w2_ref, l10_ref, l20_ref, l21_ref, d0_ref, d1_ref, d2_ref, out_ref, w3_ref, m10_ref, m2_ref, c3_ref, x_ref, s_ref,
):
    step = pl.program_id(0)
    r = place_ref[0]
    c = place_ref[1]
    part = x_ref.shape[0] // 8

    @pl.when(step == 0)
    def _():
        w3_ref[0] = right3(w0_ref[...])
        w3_ref[1] = right3(w1_ref[...])
        w3_ref[2] = right3(w2_ref[...])
        m10_ref[...] = right3(l10_ref[...])
        m2_ref[...] = right3(jnp.concatenate([l20_ref[...], l21_ref[...]], 1))
        c3_ref[...] = right3(solved_ref[...])

    for q in range(8):
        for n in range(8):
            to = n * part + 8 * q
            x_ref[to : to + 8, :] = rows_ref[q, 0, 8 * n : 8 * n + 8, :]

    s_ref[:, :BLOCK] = nt(left3(x_ref[:, :BLOCK]), w3_ref[0])

    s1 = nt(left3(x_ref[:, BLOCK : 2 * BLOCK] - nt(left3(s_ref[:, :BLOCK]), m10_ref[...])), w3_ref[1])
    s_ref[:, BLOCK : 2 * BLOCK] = s1

    s2 = nt(left3(x_ref[:, 2 * BLOCK :] - nt(left3(s_ref[:, : 2 * BLOCK]), m2_ref[...])), w3_ref[2])
    s_ref[:, 2 * BLOCK :] = s2

    rng = 2 * r + step

    @pl.when((c >= PANELS) & (rng >= PANELS))
    def _():
        total = front_ref[...]
        for q in range(NKIDS):
            cols = two(hot_t(col_hot_ref[q : q + 1, :]))
            rows = two(hot_t(row_hot_ref[step, q : q + 1, :]))
            spread_cols = nt(cols, jnp.concatenate(split2(arrived_ref[q, 0]), 1))
            total = total + nt(rows, jnp.concatenate(split2(spread_cols), 1))
        out_ref[...] = total - nt(left3(s_ref[...]), c3_ref[...])

    @pl.when((rng < jnp.minimum(c, PANELS)))
    def _():
        out_ref[...] = jnp.zeros_like(out_ref)

    for p, d_ref in enumerate((d0_ref, d1_ref, d2_ref)):
        @pl.when((c == p) & (rng > p))
        def _():
            out_ref[...] = s_ref[:, p * BLOCK : (p + 1) * BLOCK]

        @pl.when((c == p) & (rng == p))
        def _():
            pltpu.sync_copy(d_ref, out_ref)


def finish_call(place, row_rows, front, arrived, row_hot, col_hot, mats):
    return pl.pallas_call(
        finish,
        grid=(2,),
        in_specs=[
            SMEM,
            pl.BlockSpec((8, 1, BLOCK // 8, LEAD), lambda i: (0, i, 0, 0)),
            pl.BlockSpec((BLOCK, BLOCK), lambda i: (i, 0)),
            pl.BlockSpec((NKIDS, 1, PICK, PICK), lambda i: (0, i, 0, 0)),
            VMEM,
            VMEM,
        ]
        + [VMEM] * 7
        + [pl.BlockSpec(memory_space=pl.ANY)] * 3,
        out_specs=pl.BlockSpec((BLOCK, BLOCK), lambda i: (i, 0)),
        out_shape=jax.ShapeDtypeStruct(front.shape, F32),
        scratch_shapes=[
            pltpu.VMEM((3, BLOCK, 3 * BLOCK), B16),
            pltpu.VMEM((BLOCK, 3 * BLOCK), B16),
            pltpu.VMEM((BLOCK, 6 * BLOCK), B16),
            pltpu.VMEM((BLOCK, 9 * BLOCK), B16),
            pltpu.VMEM((BLOCK, LEAD), F32),
            pltpu.VMEM((BLOCK, LEAD), F32),
        ],
        compiler_params=LARGE,
        cost_estimate=pl.CostEstimate(flops=20_000_000_000, bytes_accessed=24 << 20, transcendentals=0),
    )(place, row_rows, front, arrived, row_hot, col_hot, *mats)


ROW = ("x_hi", "z")
CHIP = ("y", "x_lo")
SHAPE = (2, 4, 4, 2, 2)
COL = CHIP + ("core",)


def copies_of(a, count):
    return jnp.broadcast_to(a[None], (count,) + a.shape)


def spread(a, axis, count):
    return lax.all_to_all(copies_of(a, count), axis, 0, 0, tiled=True)


def body(root_front, contrib, index_map):
    nr = lax.axis_size(ROW)
    nc = lax.axis_size(COL)
    r = lax.axis_index(ROW)
    c = lax.axis_index(COL)
    rows_loc, cols_loc = root_front.shape
    group = nr // NKIDS
    kid = r // group
    part = r % group
    per = cols_loc // nr
    index = index_map.reshape(NKIDS, -1, PICK) - jnp.arange(CB // PICK, dtype=jnp.int32)[:, None] * BLOCK
    odd = lax.axis_index("core").reshape(1)

    def pick(kid_id, rng):
        return lax.dynamic_slice(index, (kid_id, rng, 0), (1, 1, PICK)).reshape(1, PICK)

    def swap(rows):
        return lax.ppermute(rows, "core", [(0, 1), (1, 0)])

    with jax.named_scope("slices"):
        outgoing = pl.pallas_call(
            prepare,
            grid=(1,),
            in_specs=[
                SMEM,
                VMEM,
                VMEM,
                pl.BlockSpec((2 * PICK, PICK), lambda i: (0, 0)),
                VMEM,
            ],
            out_specs=VMEM,
            out_shape=jax.ShapeDtypeStruct((cols_loc, 2 * BLOCK + PICK), F32),
            compiler_params=PARAMS,
        )(r.reshape(1), pick(kid, c), pick(kid, part), contrib, root_front)
        got = lax.all_to_all(outgoing.reshape(nr, per, -1), ROW, 0, 0, tiled=True)
        own_slice = pl.pallas_call(
            combine,
            in_specs=[VMEM, VMEM],
            out_specs=VMEM,
            out_shape=jax.ShapeDtypeStruct((per, LEAD), F32),
            compiler_params=SMALL,
        )(index[:, 2, :], got)

    with jax.named_scope("panel_cols"):
        far = lax.ppermute(own_slice, "x_hi", [(0, 1), (1, 0)])

    with jax.named_scope("lead"):
        pieces = lax.all_to_all(own_slice.reshape(nc // 2, per // (nc // 2), LEAD), CHIP, 0, 0, tiled=True)
        pieces, far, early = lax.optimization_barrier((pieces, far, own_slice))
        top, last = pieces[0], pieces[1]
        even_blocks = [top[:, :BLOCK], top[:, 2 * BLOCK :], last[:, 2 * BLOCK :]]
        odd_blocks = [top[:, BLOCK : 2 * BLOCK], top[:, :BLOCK], top[:, 2 * BLOCK :]]
        strip = jnp.where(odd[0] == 1, jnp.concatenate(odd_blocks, 1), jnp.concatenate(even_blocks, 1))
        both = jnp.concatenate([copies_of(strip, nr), pieces], 1)
        both = lax.all_to_all(both, ROW, 0, 0, tiled=True)
        strip = both[:, : pieces.shape[1]].reshape(-1, LEAD)
        share = both[:, pieces.shape[1] :].reshape(-1, LEAD)
        mine1 = spread(strip[:, :BLOCK], CHIP, nc // 2).reshape(-1, BLOCK)
        other1 = swap(mine1)
        fan = copies_of(strip[:, BLOCK:], nc // 2)
        mine1, other1, fan = lax.optimization_barrier((mine1, other1, fan))
        mine2 = lax.all_to_all(fan, CHIP, 0, 0, tiled=True).reshape(-1, 2 * BLOCK)

    with jax.named_scope("panel_cols"):
        high = lax.axis_index("x_hi") == 1
        pair = jnp.stack([jnp.where(high, far, early), jnp.where(high, early, far)])
        col_rows = lax.all_gather(pair, "z", axis=0, tiled=False)

    with jax.named_scope("factor"):
        l00, w0 = factor_call(factor0, 2, 1, odd, mine1, other1)

    with jax.named_scope("panel_rows"):
        w0, contrib, mine2, share = lax.optimization_barrier((w0, contrib, mine2, share))
        other2 = swap(mine2)
        row_rows = lax.all_gather(share, COL, axis=0, tiled=False)
        row_rows = row_rows.reshape(nc // 2, 2, per, LEAD)

    with jax.named_scope("exchange"):
        arrived = lax.all_to_all(contrib.reshape(nr, PICK, PICK), ROW, 0, 0, tiled=True)

    with jax.named_scope("factor"):
        l11, w1, l10 = factor_call(factor1, 3, 2, odd, mine1, other1, mine2, other2, w0)
        l22, w2, l20, l21 = factor_call(factor2, 4, 3, odd, mine2, other2, w0, w1, l10)

    with jax.named_scope("finish"):
        mats = (w0, w1, w2, l10, l20, l21)
        solved = solve_cols_call(col_rows, mats)
        row_hot = lax.dynamic_slice(index, (0, group * r, 0), (NKIDS, group, PICK)).transpose(1, 0, 2)
        col_hot = lax.dynamic_slice(index, (0, c, 0), (NKIDS, 1, PICK)).reshape(NKIDS, PICK)
        return finish_call(
            jnp.stack([r, c]),
            row_rows,
            root_front,
            arrived.reshape(NKIDS, group, PICK, PICK),
            row_hot,
            col_hot,
            (solved, *mats, l00, l11, l22),
        )


def solution(mesh):
    torus = Mesh(mesh.devices.reshape(SHAPE), ROW + COL)
    placed = (P(ROW, COL), P(ROW, COL), P())
    return jax.shard_map(
        body, mesh=torus, in_specs=placed, out_specs=P(ROW, COL), check_vma=False
    )
```

```python
import jax
import jax.numpy as jnp
from jax import lax
from jax.experimental import pallas as pl
from jax.experimental.pallas import tpu as pltpu
from jax.sharding import Mesh, PartitionSpec as P

CB = 4096
NKIDS = 4
BLOCK = 512
PANELS = 3
PICK = 256
LEAD = BLOCK * PANELS
F32 = jnp.float32
B16 = jnp.bfloat16


def split3(x):
    high = x.astype(B16).astype(F32)
    rest = x - high
    mid = rest.astype(B16).astype(F32)
    return high, mid, rest - mid


def outer_update(lhs, rhs):
    a_high, a_mid, a_low = split3(lhs)
    b_high, b_mid, b_low = split3(rhs)
    a = jnp.concatenate([a_high, a_high, a_mid, a_high, a_low, a_mid], 0).astype(B16)
    b = jnp.concatenate([b_high, b_mid, b_high, b_low, b_high, b_mid], 0).astype(B16)
    return lax.dot_general(a, b, (((0,), (0,)), ((), ())), preferred_element_type=F32)


def factor_tile(rows):
    count = len(rows)
    lane = lax.broadcasted_iota(jnp.int32, (8, 128), 1)
    sub = lax.broadcasted_iota(jnp.int32, (8, 128), 0)
    wide = lambda x: jnp.broadcast_to(x, (8, 128))
    rows = list(rows)
    uppers, inverses = [], []
    for k in range(count):
        c0 = 8 * k
        own = (lane >= c0) & (lane < c0 + 8)
        cur = rows[k]
        top = [wide(cur[:, c0 + j : c0 + j + 1]) for j in range(8)]
        near = range(k + 1, min(k + 3, count))
        lows = [[wide(rows[n][:, c0 + j : c0 + j + 1]) for j in range(8)] for n in near]
        afters = [jnp.where(own, 0.0, rows[n]) for n in near]
        upper = cur
        inv = jnp.where(own, jnp.where(lane - c0 == sub, 1.0, 0.0), cur)
        for j in range(8):
            scale = lax.rsqrt(wide(top[j][j : j + 1, :]))
            mult = jnp.where(sub > j, top[j] * scale, 0.0)
            low_mults = [low[j] * scale for low in lows]
            for m in range(j + 1, 8):
                u = wide(top[m][j : j + 1, :]) * scale
                top[m] = top[m] - mult * u
                for low, low_mult in zip(lows, low_mults):
                    low[m] = low[m] - low_mult * u
            u = wide(upper[j : j + 1, :]) * scale
            upper = jnp.where(sub == j, u, upper - mult * u)
            u = wide(inv[j : j + 1, :]) * scale
            inv = jnp.where(sub == j, u, inv - mult * u)
            afters = [after - low_mult * u for after, low_mult in zip(afters, low_mults)]
        uppers.append(jnp.where(lane - c0 >= sub, upper, 0.0))
        inverses.append(jnp.where(lane < c0 + 8, inv, 0.0))
        for n, after in zip(near, afters):
            rows[n] = after
        if k + 3 < count:
            update = outer_update(jnp.where(lane >= c0 + 24, upper, 0.0), inv)
            for i in range(k + 3, count):
                rows[i] = jnp.where(own, 0.0, rows[i]) - update[8 * i : 8 * i + 8, :]
    return uppers, inverses


def mm(a, b, flip=False):
    dims = (((1,), (1 if flip else 0,)), ((), ()))
    return lax.dot_general(a, b, dims, precision=lax.Precision.HIGHEST, preferred_element_type=F32)


def nt(a, b):
    return lax.dot_general(a, b, (((1,), (1,)), ((), ())), preferred_element_type=F32)


def split2(x):
    high = x.astype(B16)
    return high, (x - high.astype(F32)).astype(B16)


def left3(x):
    high, low = split2(x)
    return jnp.concatenate([high, high, low], 1)


def right3(x):
    high, low = split2(x)
    return jnp.concatenate([high, low, high], 1)


def mm3(a, b):
    return nt(left3(a), right3(b))


def whole(x):
    high, mid, low = split3(x)
    return jnp.concatenate([high, mid, low], 1).astype(B16)


def factor_block(l_ref, w_ref, s_ref):
    size = s_ref.shape[0]
    tiles = size // 128
    l_ref[...] = jnp.zeros_like(l_ref)
    w_ref[...] = jnp.zeros_like(w_ref)
    for k in range(tiles):
        o = 128 * k
        e = o + 128
        rows = [s_ref[o + 8 * i : o + 8 * i + 8, o:e] for i in range(16)]
        uppers, inverses = factor_tile(rows)
        inv = jnp.concatenate(inverses, 0)
        l_ref[o:e, o:e] = jnp.concatenate(uppers, 0).T
        w_ref[o:e, o:e] = inv
        if k + 1 < tiles:
            below = mm(s_ref[e:, o:e], inv, True)
            l_ref[e:, o:e] = below
            s_ref[e:, e:] = s_ref[e:, e:] - mm(below, below, True)
    half = 128
    while half < size:
        for o in range(0, size, 2 * half):
            m = o + half
            e = m + half
            t = mm(l_ref[m:e, o:m], w_ref[o:m, o:m])
            w_ref[m:e, o:m] = -mm(w_ref[m:e, m:e], t)
        half *= 2


def put_rows(dst, a_ref, b_ref, second, col):
    for q in range(8):
        for i in range(8):
            src = slice(64 * q + 8 * i, 64 * q + 8 * i + 8)
            cols = slice(col, col + BLOCK)
            dst[64 * i + 8 * q : 64 * i + 8 * q + 8, :] = jnp.where(second, b_ref[src, cols], a_ref[src, cols])


def factor0(odd_ref, mine_ref, other_ref, l_ref, w_ref, s_ref):
    put_rows(s_ref, mine_ref, other_ref, odd_ref[0] == 1, 0)
    factor_block(l_ref, w_ref, s_ref)


def factor1(odd_ref, mine1_ref, other1_ref, mine2_ref, other2_ref, w0_ref, l_ref, w_ref, l10_ref, s_ref, x_ref):
    even = odd_ref[0] == 0
    put_rows(x_ref, mine2_ref, other2_ref, even, 0)
    put_rows(s_ref, mine1_ref, other1_ref, even, 0)
    l10 = mm3(x_ref[...], w0_ref[...])
    l10_ref[...] = l10
    s_ref[...] = s_ref[...] - mm3(l10, l10)
    factor_block(l_ref, w_ref, s_ref)


def factor2(
    odd_ref, mine_ref, other_ref, w0_ref, w1_ref, l10_ref, cols_ref,
    l_ref, w_ref, l20_ref, l21_ref, solved_ref, s_ref, x_ref, y_ref, c_ref, sem,
):
    copy = pltpu.make_async_copy(cols_ref, c_ref, sem)
    copy.start()
    odd = odd_ref[0] == 1
    put_rows(x_ref, mine_ref, other_ref, odd, 0)
    put_rows(y_ref, mine_ref, other_ref, jnp.logical_not(odd), BLOCK)
    put_rows(s_ref, mine_ref, other_ref, odd, BLOCK)
    l20 = mm3(x_ref[...].T, w0_ref[...])
    l20_ref[...] = l20
    l21 = mm3(y_ref[...].T - mm3(l20, l10_ref[...]), w1_ref[...])
    l21_ref[...] = l21
    both = jnp.concatenate([l20, l21], 1)
    s_ref[...] = s_ref[...] - mm3(both, both)
    factor_block(l_ref, w_ref, s_ref)

    copy.wait()
    part = BLOCK // 8

    def rows(p):
        cols = slice(p * BLOCK, (p + 1) * BLOCK)
        for n in range(8):
            x_ref[n * part : (n + 1) * part, :] = c_ref[n % 4, n // 4, :, cols]
        return x_ref[...]

    s0 = mm3(rows(0), w0_ref[...])
    solved_ref[:, :BLOCK] = s0
    s1 = mm3(rows(1) - mm3(s0, l10_ref[...]), w1_ref[...])
    solved_ref[:, BLOCK : 2 * BLOCK] = s1
    early = mm3(s0, l20_ref[...]) + mm3(s1, l21_ref[...])
    solved_ref[:, 2 * BLOCK :] = mm3(rows(2) - early, w_ref[...])


VMEM = pl.BlockSpec(memory_space=pltpu.VMEM)
SMEM = pl.BlockSpec(memory_space=pltpu.SMEM)
PARAMS = pltpu.CompilerParams(vmem_limit_bytes=60 << 20)
SMALL = pltpu.CompilerParams(vmem_limit_bytes=16 << 20)


SQUARE = jax.ShapeDtypeStruct((BLOCK, BLOCK), F32)


def factor_call(kernel, outs, scratch, *args):
    specs = [pl.BlockSpec(memory_space=pl.ANY) if x.ndim > 2 else pl.BlockSpec(x.shape, lambda i: (0, 0)) for x in args[1:]]
    return pl.pallas_call(
        kernel,
        grid=(1,),
        in_specs=[SMEM] + specs,
        out_specs=[pl.BlockSpec(x.shape, lambda i: (0, 0)) for x in outs],
        out_shape=outs,
        scratch_shapes=scratch,
        compiler_params=PARAMS,
        cost_estimate=pl.CostEstimate(flops=20_000_000_000, bytes_accessed=1 << 24, transcendentals=0),
    )(*args)


def hot_t(index, size=BLOCK):
    place = lax.broadcasted_iota(jnp.int32, (size, index.shape[1]), 0)
    return (place == index).astype(F32).astype(B16)


def three(x):
    return jnp.concatenate([x, x, x], 1)


def prepare(flag_ref, cols_ref, rows_ref, contrib_ref, root_ref, out_ref):
    cols = three(hot_t(cols_ref[...]))
    rows = three(hot_t(rows_ref[...]))
    first = nt(whole(nt(cols, whole(contrib_ref[:PICK, :]))), rows)
    third = nt(cols, whole(contrib_ref[PICK:, :]))
    root_a = root_ref[:BLOCK, :].T
    root_b = root_ref[BLOCK:, :].T
    is_first = flag_ref[0] == 0
    out_ref[:, :BLOCK] = first + jnp.where(is_first, root_a, 0.0)
    out_ref[:, BLOCK : 2 * BLOCK] = jnp.where(is_first, root_b, root_a)
    out_ref[:, 2 * BLOCK :] = third


def combine(index_ref, got_ref, out_ref):
    first = lambda n: got_ref[n, :, :BLOCK]
    out_ref[:, :BLOCK] = (first(0) + first(2)) + (first(4) + first(6))
    out_ref[:, BLOCK : 2 * BLOCK] = (
        (first(1) + first(3)) + (first(5) + first(7)) + got_ref[0, :, BLOCK : 2 * BLOCK]
    )
    total = got_ref[1, :, BLOCK : 2 * BLOCK]
    for q in range(NKIDS):
        rows = three(hot_t(index_ref[q : q + 1, :]))
        total = total + nt(whole(got_ref[2 * q, :, 2 * BLOCK :]), rows)
    out_ref[:, 2 * BLOCK :] = total


def two(x):
    return jnp.concatenate([x, x], 1)


def finish(
    place_ref, rows_ref, front_ref, arrived_ref, row_hot_ref, col_hot_ref,
    solved_ref, w0_ref, w1_ref, w2_ref, l10_ref, l20_ref, l21_ref, d0_ref, d1_ref, d2_ref, out_ref, w3_ref, m10_ref, m2_ref, c3_ref, x_ref, s_ref, raw_ref, cols_ref, sem,
):
    step = pl.program_id(0)
    r = place_ref[0]
    c = place_ref[1]
    part = x_ref.shape[0] // 8
    sources = (w0_ref, l10_ref, w1_ref, l20_ref, l21_ref, w2_ref)
    copies = [
        pltpu.make_async_copy(src, raw_ref.at[n], sem.at[n]) for n, src in enumerate(sources)
    ] + [pltpu.make_async_copy(solved_ref, cols_ref, sem.at[len(sources)])]

    @pl.when(step == 0)
    def _():
        for copy in copies:
            copy.start()

    for q in range(8):
        for n in range(8):
            to = n * part + 8 * q
            x_ref[to : to + 8, :] = rows_ref[q, 0, 8 * n : 8 * n + 8, :]

    @pl.when(step == 0)
    def _():
        copies[0].wait()
        w3_ref[0] = right3(raw_ref[0])

    s_ref[:, :BLOCK] = nt(left3(x_ref[:, :BLOCK]), w3_ref[0])

    @pl.when(step == 0)
    def _():
        copies[1].wait()
        m10_ref[...] = right3(raw_ref[1])
        copies[2].wait()
        w3_ref[1] = right3(raw_ref[2])

    s1 = nt(left3(x_ref[:, BLOCK : 2 * BLOCK] - nt(left3(s_ref[:, :BLOCK]), m10_ref[...])), w3_ref[1])
    s_ref[:, BLOCK : 2 * BLOCK] = s1

    @pl.when(step == 0)
    def _():
        copies[3].wait()
        copies[4].wait()
        m2_ref[...] = right3(jnp.concatenate([raw_ref[3], raw_ref[4]], 1))
        copies[5].wait()
        w3_ref[2] = right3(raw_ref[5])

    s2 = nt(left3(x_ref[:, 2 * BLOCK :] - nt(left3(s_ref[:, : 2 * BLOCK]), m2_ref[...])), w3_ref[2])
    s_ref[:, 2 * BLOCK :] = s2

    @pl.when(step == 0)
    def _():
        copies[6].wait()
        c3_ref[...] = right3(cols_ref[...])

    rng = 2 * r + step

    @pl.when((c >= PANELS) & (rng >= PANELS))
    def _():
        total = front_ref[...]
        for q in range(NKIDS):
            cols = two(hot_t(col_hot_ref[q : q + 1, :]))
            rows = two(hot_t(row_hot_ref[step, q : q + 1, :]))
            spread_cols = nt(cols, jnp.concatenate(split2(arrived_ref[q, 0]), 1))
            total = total + nt(rows, jnp.concatenate(split2(spread_cols), 1))
        out_ref[...] = total - nt(left3(s_ref[...]), c3_ref[...])

    @pl.when((rng < jnp.minimum(c, PANELS)))
    def _():
        out_ref[...] = jnp.zeros_like(out_ref)

    for p, d_ref in enumerate((d0_ref, d1_ref, d2_ref)):
        @pl.when((c == p) & (rng > p))
        def _():
            out_ref[...] = s_ref[:, p * BLOCK : (p + 1) * BLOCK]

        @pl.when((c == p) & (rng == p))
        def _():
            pltpu.sync_copy(d_ref, out_ref)


def finish_call(place, row_rows, front, arrived, row_hot, col_hot, mats):
    return pl.pallas_call(
        finish,
        grid=(2,),
        in_specs=[
            SMEM,
            pl.BlockSpec((8, 1, BLOCK // 8, LEAD), lambda i: (0, i, 0, 0)),
            pl.BlockSpec((BLOCK, BLOCK), lambda i: (i, 0)),
            pl.BlockSpec((NKIDS, 1, PICK, PICK), lambda i: (0, i, 0, 0)),
            VMEM,
            VMEM,
        ]
        + [pl.BlockSpec(memory_space=pl.ANY)] * 10,
        out_specs=pl.BlockSpec((BLOCK, BLOCK), lambda i: (i, 0)),
        out_shape=jax.ShapeDtypeStruct(front.shape, F32),
        scratch_shapes=[
            pltpu.VMEM((3, BLOCK, 3 * BLOCK), B16),
            pltpu.VMEM((BLOCK, 3 * BLOCK), B16),
            pltpu.VMEM((BLOCK, 6 * BLOCK), B16),
            pltpu.VMEM((BLOCK, 9 * BLOCK), B16),
            pltpu.VMEM((BLOCK, LEAD), F32),
            pltpu.VMEM((BLOCK, LEAD), F32),
            pltpu.VMEM((6, BLOCK, BLOCK), F32),
            pltpu.VMEM((BLOCK, LEAD), F32),
            pltpu.SemaphoreType.DMA((7,)),
        ],
        compiler_params=PARAMS,
        cost_estimate=pl.CostEstimate(flops=20_000_000_000, bytes_accessed=24 << 20, transcendentals=0),
    )(place, row_rows, front, arrived, row_hot, col_hot, *mats)


ROW = ("x_hi", "z")
CHIP = ("y", "x_lo")
SHAPE = (2, 4, 4, 2, 2)
COL = CHIP + ("core",)


def copies_of(a, count):
    return jnp.broadcast_to(a[None], (count,) + a.shape)


def spread(a, axis, count):
    return lax.all_to_all(copies_of(a, count), axis, 0, 0, tiled=True)


def body(root_front, contrib, index_map):
    nr = lax.axis_size(ROW)
    nc = lax.axis_size(COL)
    r = lax.axis_index(ROW)
    c = lax.axis_index(COL)
    rows_loc, cols_loc = root_front.shape
    group = nr // NKIDS
    kid = r // group
    part = r % group
    per = cols_loc // nr
    index = index_map.reshape(NKIDS, -1, PICK) - jnp.arange(CB // PICK, dtype=jnp.int32)[:, None] * BLOCK
    odd = lax.axis_index("core").reshape(1)

    def pick(kid_id, rng):
        return lax.dynamic_slice(index, (kid_id, rng, 0), (1, 1, PICK)).reshape(1, PICK)

    def swap(rows):
        return lax.ppermute(rows, "core", [(0, 1), (1, 0)])

    with jax.named_scope("slices"):
        outgoing = pl.pallas_call(
            prepare,
            grid=(1,),
            in_specs=[
                SMEM,
                VMEM,
                VMEM,
                pl.BlockSpec((2 * PICK, PICK), lambda i: (0, 0)),
                VMEM,
            ],
            out_specs=VMEM,
            out_shape=jax.ShapeDtypeStruct((cols_loc, 2 * BLOCK + PICK), F32),
            compiler_params=PARAMS,
        )(r.reshape(1), pick(kid, c), pick(kid, part), contrib, root_front)
        got = lax.all_to_all(outgoing.reshape(nr, per, -1), ROW, 0, 0, tiled=True)
        own_slice = pl.pallas_call(
            combine,
            in_specs=[VMEM, VMEM],
            out_specs=VMEM,
            out_shape=jax.ShapeDtypeStruct((per, LEAD), F32),
            compiler_params=SMALL,
        )(index[:, 2, :], got)

    with jax.named_scope("panel_cols"):
        far = lax.ppermute(own_slice, "x_hi", [(0, 1), (1, 0)])

    with jax.named_scope("lead"):
        pieces = lax.all_to_all(own_slice.reshape(nc // 2, per // (nc // 2), LEAD), CHIP, 0, 0, tiled=True)
        pieces, far, early = lax.optimization_barrier((pieces, far, own_slice))
        top, last = pieces[0], pieces[1]
        even_blocks = [top[:, :BLOCK], top[:, 2 * BLOCK :], last[:, 2 * BLOCK :]]
        odd_blocks = [top[:, BLOCK : 2 * BLOCK], top[:, :BLOCK], top[:, 2 * BLOCK :]]
        strip = jnp.where(odd[0] == 1, jnp.concatenate(odd_blocks, 1), jnp.concatenate(even_blocks, 1))
        both = jnp.concatenate([copies_of(strip, nr), pieces], 1)
        both = lax.all_to_all(both, ROW, 0, 0, tiled=True)
        strip = both[:, : pieces.shape[1]].reshape(-1, LEAD)
        share = both[:, pieces.shape[1] :].reshape(-1, LEAD)
        mine1 = spread(strip[:, :BLOCK], CHIP, nc // 2).reshape(-1, BLOCK)
        other1 = swap(mine1)
        fan = copies_of(strip[:, BLOCK:], nc // 2)
        mine1, other1, fan = lax.optimization_barrier((mine1, other1, fan))
        mine2 = lax.all_to_all(fan, CHIP, 0, 0, tiled=True).reshape(-1, 2 * BLOCK)

    with jax.named_scope("panel_cols"):
        high = lax.axis_index("x_hi") == 1
        pair = jnp.stack([jnp.where(high, far, early), jnp.where(high, early, far)])
        col_rows = lax.all_gather(pair, "z", axis=0, tiled=False)

    with jax.named_scope("factor"):
        square = pltpu.VMEM((BLOCK, BLOCK), F32)
        l00, w0 = factor_call(factor0, [SQUARE] * 2, [square], odd, mine1, other1)

    with jax.named_scope("panel_rows"):
        w0, contrib, mine2, share = lax.optimization_barrier((w0, contrib, mine2, share))
        other2 = swap(mine2)
        row_rows = lax.all_gather(share, COL, axis=0, tiled=False)
        row_rows = row_rows.reshape(nc // 2, 2, per, LEAD)

    with jax.named_scope("exchange"):
        arrived = lax.all_to_all(contrib.reshape(nr, PICK, PICK), ROW, 0, 0, tiled=True)

    with jax.named_scope("factor"):
        l11, w1, l10 = factor_call(
            factor1, [SQUARE] * 3, [square] * 2, odd, mine1, other1, mine2, other2, w0
        )
        l22, w2, l20, l21, solved = factor_call(
            factor2,
            [SQUARE] * 4 + [jax.ShapeDtypeStruct((cols_loc, LEAD), F32)],
            [square] * 3 + [pltpu.VMEM(col_rows.shape, F32), pltpu.SemaphoreType.DMA],
            odd, mine2, other2, w0, w1, l10, col_rows,
        )

    with jax.named_scope("finish"):
        mats = (w0, w1, w2, l10, l20, l21)
        row_hot = lax.dynamic_slice(index, (0, group * r, 0), (NKIDS, group, PICK)).transpose(1, 0, 2)
        col_hot = lax.dynamic_slice(index, (0, c, 0), (NKIDS, 1, PICK)).reshape(NKIDS, PICK)
        return finish_call(
            jnp.stack([r, c]),
            row_rows,
            root_front,
            arrived.reshape(NKIDS, group, PICK, PICK),
            row_hot,
            col_hot,
            (solved, *mats, l00, l11, l22),
        )


def solution(mesh):
    torus = Mesh(mesh.devices.reshape(SHAPE), ROW + COL)
    placed = (P(ROW, COL), P(ROW, COL), P())
    return jax.shard_map(
        body, mesh=torus, in_specs=placed, out_specs=P(ROW, COL), check_vma=False
    )
```

```python
import jax
import jax.numpy as jnp
from jax import lax
from jax.experimental import pallas as pl
from jax.experimental.pallas import tpu as pltpu
from jax.sharding import Mesh, PartitionSpec as P

CB = 4096
NKIDS = 4
BLOCK = 512
PANELS = 3
PICK = 256
LEAD = BLOCK * PANELS
F32 = jnp.float32
B16 = jnp.bfloat16


def split3(x):
    high = x.astype(B16).astype(F32)
    rest = x - high
    mid = rest.astype(B16).astype(F32)
    return high, mid, rest - mid


def outer_update(lhs, rhs):
    a_high, a_mid, a_low = split3(lhs)
    b_high, b_mid, b_low = split3(rhs)
    a = jnp.concatenate([a_high, a_high, a_mid, a_high, a_low, a_mid], 0).astype(B16)
    b = jnp.concatenate([b_high, b_mid, b_high, b_low, b_high, b_mid], 0).astype(B16)
    return lax.dot_general(a, b, (((0,), (0,)), ((), ())), preferred_element_type=F32)


def factor_tile(rows):
    count = len(rows)
    lane = lax.broadcasted_iota(jnp.int32, (8, 128), 1)
    sub = lax.broadcasted_iota(jnp.int32, (8, 128), 0)
    wide = lambda x: jnp.broadcast_to(x, (8, 128))
    rows = list(rows)
    uppers, inverses = [], []
    for k in range(count):
        c0 = 8 * k
        own = (lane >= c0) & (lane < c0 + 8)
        cur = rows[k]
        top = [wide(cur[:, c0 + j : c0 + j + 1]) for j in range(8)]
        near = range(k + 1, min(k + 3, count))
        lows = [[wide(rows[n][:, c0 + j : c0 + j + 1]) for j in range(8)] for n in near]
        afters = [jnp.where(own, 0.0, rows[n]) for n in near]
        upper = cur
        inv = jnp.where(own, jnp.where(lane - c0 == sub, 1.0, 0.0), cur)
        for j in range(8):
            scale = lax.rsqrt(wide(top[j][j : j + 1, :]))
            mult = jnp.where(sub > j, top[j] * scale, 0.0)
            low_mults = [low[j] * scale for low in lows]
            for m in range(j + 1, 8):
                u = wide(top[m][j : j + 1, :]) * scale
                top[m] = top[m] - mult * u
                for low, low_mult in zip(lows, low_mults):
                    low[m] = low[m] - low_mult * u
            u = wide(upper[j : j + 1, :]) * scale
            upper = jnp.where(sub == j, u, upper - mult * u)
            u = wide(inv[j : j + 1, :]) * scale
            inv = jnp.where(sub == j, u, inv - mult * u)
            afters = [after - low_mult * u for after, low_mult in zip(afters, low_mults)]
        uppers.append(jnp.where(lane - c0 >= sub, upper, 0.0))
        inverses.append(jnp.where(lane < c0 + 8, inv, 0.0))
        for n, after in zip(near, afters):
            rows[n] = after
        if k + 3 < count:
            update = outer_update(jnp.where(lane >= c0 + 24, upper, 0.0), inv)
            for i in range(k + 3, count):
                rows[i] = jnp.where(own, 0.0, rows[i]) - update[8 * i : 8 * i + 8, :]
    return uppers, inverses


def mm(a, b, flip=False):
    a_high, a_mid, a_low = (x.astype(B16) for x in split3(a))
    b_high, b_mid, b_low = (x.astype(B16) for x in split3(b))
    left = jnp.concatenate([a_high, a_high, a_mid, a_high, a_low, a_mid], 1)
    right = [b_high, b_mid, b_high, b_low, b_high, b_mid]
    if flip:
        return nt(left, jnp.concatenate(right, 1))
    return nn(left, jnp.concatenate(right, 0))


def nn(a, b):
    return lax.dot_general(a, b, (((1,), (0,)), ((), ())), preferred_element_type=F32)


def nt(a, b):
    return lax.dot_general(a, b, (((1,), (1,)), ((), ())), preferred_element_type=F32)


def split2(x):
    high = x.astype(B16)
    return high, (x - high.astype(F32)).astype(B16)


def left3(x):
    high, low = split2(x)
    return jnp.concatenate([high, high, low], 1)


def right3(x):
    high, low = split2(x)
    return jnp.concatenate([high, low, high], 1)


def mm3(a, b):
    return nt(left3(a), right3(b))


def whole(x):
    high, mid, low = split3(x)
    return jnp.concatenate([high, mid, low], 1).astype(B16)


def factor_block(l_ref, w_ref, s_ref):
    size = s_ref.shape[0]
    tiles = size // 128
    l_ref[...] = jnp.zeros_like(l_ref)
    w_ref[...] = jnp.zeros_like(w_ref)
    for k in range(tiles):
        o = 128 * k
        e = o + 128
        rows = [s_ref[o + 8 * i : o + 8 * i + 8, o:e] for i in range(16)]
        uppers, inverses = factor_tile(rows)
        inv = jnp.concatenate(inverses, 0)
        l_ref[o:e, o:e] = jnp.concatenate(uppers, 0).T
        w_ref[o:e, o:e] = inv
        if k + 1 < tiles:
            below = mm(s_ref[e:, o:e], inv, True)
            l_ref[e:, o:e] = below
            s_ref[e:, e:] = s_ref[e:, e:] - mm(below, below, True)
    half = 128
    while half < size:
        for o in range(0, size, 2 * half):
            m = o + half
            e = m + half
            t = mm(l_ref[m:e, o:m], w_ref[o:m, o:m])
            w_ref[m:e, o:m] = -mm(w_ref[m:e, m:e], t)
        half *= 2


def put_rows(dst, a_ref, b_ref, second, col):
    for q in range(8):
        for i in range(8):
            src = slice(64 * q + 8 * i, 64 * q + 8 * i + 8)
            cols = slice(col, col + BLOCK)
            dst[64 * i + 8 * q : 64 * i + 8 * q + 8, :] = jnp.where(second, b_ref[src, cols], a_ref[src, cols])


def factor0(odd_ref, mine_ref, other_ref, l_ref, w_ref, s_ref):
    put_rows(s_ref, mine_ref, other_ref, odd_ref[0] == 1, 0)
    factor_block(l_ref, w_ref, s_ref)


def factor1(odd_ref, mine1_ref, other1_ref, mine2_ref, other2_ref, w0_ref, l_ref, w_ref, l10_ref, s_ref, x_ref):
    even = odd_ref[0] == 0
    put_rows(x_ref, mine2_ref, other2_ref, even, 0)
    put_rows(s_ref, mine1_ref, other1_ref, even, 0)
    l10 = mm3(x_ref[...], w0_ref[...])
    l10_ref[...] = l10
    s_ref[...] = s_ref[...] - mm3(l10, l10)
    factor_block(l_ref, w_ref, s_ref)


def factor2(
    odd_ref, mine_ref, other_ref, w0_ref, w1_ref, l10_ref, cols_ref,
    l_ref, w_ref, l20_ref, l21_ref, solved_ref, s_ref, x_ref, y_ref, c_ref, sem,
):
    copy = pltpu.make_async_copy(cols_ref, c_ref, sem)
    copy.start()
    odd = odd_ref[0] == 1
    put_rows(x_ref, mine_ref, other_ref, odd, 0)
    put_rows(y_ref, mine_ref, other_ref, jnp.logical_not(odd), BLOCK)
    put_rows(s_ref, mine_ref, other_ref, odd, BLOCK)
    l20 = mm3(x_ref[...].T, w0_ref[...])
    l20_ref[...] = l20
    l21 = mm3(y_ref[...].T - mm3(l20, l10_ref[...]), w1_ref[...])
    l21_ref[...] = l21
    both = jnp.concatenate([l20, l21], 1)
    s_ref[...] = s_ref[...] - mm3(both, both)
    factor_block(l_ref, w_ref, s_ref)

    copy.wait()
    part = BLOCK // 8

    def rows(p):
        cols = slice(p * BLOCK, (p + 1) * BLOCK)
        for n in range(8):
            x_ref[n * part : (n + 1) * part, :] = c_ref[n % 4, n // 4, :, cols]
        return x_ref[...]

    s0 = mm3(rows(0), w0_ref[...])
    solved_ref[:, :BLOCK] = s0
    s1 = mm3(rows(1) - mm3(s0, l10_ref[...]), w1_ref[...])
    solved_ref[:, BLOCK : 2 * BLOCK] = s1
    early = mm3(s0, l20_ref[...]) + mm3(s1, l21_ref[...])
    solved_ref[:, 2 * BLOCK :] = mm3(rows(2) - early, w_ref[...])


VMEM = pl.BlockSpec(memory_space=pltpu.VMEM)
SMEM = pl.BlockSpec(memory_space=pltpu.SMEM)
PARAMS = pltpu.CompilerParams(vmem_limit_bytes=60 << 20)
SMALL = pltpu.CompilerParams(vmem_limit_bytes=16 << 20)


SQUARE = jax.ShapeDtypeStruct((BLOCK, BLOCK), F32)


def factor_call(kernel, outs, scratch, *args):
    specs = [pl.BlockSpec(memory_space=pl.ANY) if x.ndim > 2 else pl.BlockSpec(x.shape, lambda i: (0, 0)) for x in args[1:]]
    return pl.pallas_call(
        kernel,
        grid=(1,),
        in_specs=[SMEM] + specs,
        out_specs=[pl.BlockSpec(x.shape, lambda i: (0, 0)) for x in outs],
        out_shape=outs,
        scratch_shapes=scratch,
        compiler_params=PARAMS,
        cost_estimate=pl.CostEstimate(flops=20_000_000_000, bytes_accessed=1 << 24, transcendentals=0),
    )(*args)


def hot_t(index, size=BLOCK):
    place = lax.broadcasted_iota(jnp.int32, (size, index.shape[1]), 0)
    return (place == index).astype(F32).astype(B16)


def three(x):
    return jnp.concatenate([x, x, x], 1)


def prepare(flag_ref, cols_ref, rows_ref, contrib_ref, root_ref, out_ref):
    cols = three(hot_t(cols_ref[...]))
    rows = three(hot_t(rows_ref[...]))
    first = nt(whole(nt(cols, whole(contrib_ref[:PICK, :]))), rows)
    third = nt(cols, whole(contrib_ref[PICK:, :]))
    root_a = root_ref[:BLOCK, :].T
    root_b = root_ref[BLOCK:, :].T
    is_first = flag_ref[0] == 0
    out_ref[:, :BLOCK] = first + jnp.where(is_first, root_a, 0.0)
    out_ref[:, BLOCK : 2 * BLOCK] = jnp.where(is_first, root_b, root_a)
    out_ref[:, 2 * BLOCK :] = third


def combine(index_ref, got_ref, out_ref):
    first = lambda n: got_ref[n, :, :BLOCK]
    out_ref[:, :BLOCK] = (first(0) + first(2)) + (first(4) + first(6))
    out_ref[:, BLOCK : 2 * BLOCK] = (
        (first(1) + first(3)) + (first(5) + first(7)) + got_ref[0, :, BLOCK : 2 * BLOCK]
    )
    total = got_ref[1, :, BLOCK : 2 * BLOCK]
    for q in range(NKIDS):
        rows = three(hot_t(index_ref[q : q + 1, :]))
        total = total + nt(whole(got_ref[2 * q, :, 2 * BLOCK :]), rows)
    out_ref[:, 2 * BLOCK :] = total


def two(x):
    return jnp.concatenate([x, x], 1)


def finish(
    place_ref, rows_ref, front_ref, arrived_ref, row_hot_ref, col_hot_ref,
    solved_ref, w0_ref, w1_ref, w2_ref, l10_ref, l20_ref, l21_ref, d0_ref, d1_ref, d2_ref, out_ref, w3_ref, m10_ref, m2_ref, c3_ref, x_ref, s_ref, raw_ref, cols_ref, sem,
):
    step = pl.program_id(0)
    r = place_ref[0]
    c = place_ref[1]
    part = x_ref.shape[0] // 8
    sources = (w0_ref, l10_ref, w1_ref, l20_ref, l21_ref, w2_ref)
    copies = [
        pltpu.make_async_copy(src, raw_ref.at[n], sem.at[n]) for n, src in enumerate(sources)
    ] + [pltpu.make_async_copy(solved_ref, cols_ref, sem.at[len(sources)])]

    @pl.when(step == 0)
    def _():
        for copy in copies:
            copy.start()

    for q in range(8):
        for n in range(8):
            to = n * part + 8 * q
            x_ref[to : to + 8, :] = rows_ref[q, 0, 8 * n : 8 * n + 8, :]

    @pl.when(step == 0)
    def _():
        copies[0].wait()
        w3_ref[0] = right3(raw_ref[0])

    s_ref[:, :BLOCK] = nt(left3(x_ref[:, :BLOCK]), w3_ref[0])

    @pl.when(step == 0)
    def _():
        copies[1].wait()
        m10_ref[...] = right3(raw_ref[1])
        copies[2].wait()
        w3_ref[1] = right3(raw_ref[2])

    s1 = nt(left3(x_ref[:, BLOCK : 2 * BLOCK] - nt(left3(s_ref[:, :BLOCK]), m10_ref[...])), w3_ref[1])
    s_ref[:, BLOCK : 2 * BLOCK] = s1

    @pl.when(step == 0)
    def _():
        copies[3].wait()
        copies[4].wait()
        m2_ref[...] = right3(jnp.concatenate([raw_ref[3], raw_ref[4]], 1))
        copies[5].wait()
        w3_ref[2] = right3(raw_ref[5])

    s2 = nt(left3(x_ref[:, 2 * BLOCK :] - nt(left3(s_ref[:, : 2 * BLOCK]), m2_ref[...])), w3_ref[2])
    s_ref[:, 2 * BLOCK :] = s2

    @pl.when(step == 0)
    def _():
        copies[6].wait()
        c3_ref[...] = right3(cols_ref[...])

    rng = 2 * r + step

    @pl.when((c >= PANELS) & (rng >= PANELS))
    def _():
        total = front_ref[...]
        for q in range(NKIDS):
            cols = two(hot_t(col_hot_ref[q : q + 1, :]))
            rows = two(hot_t(row_hot_ref[step, q : q + 1, :]))
            spread_cols = nt(cols, jnp.concatenate(split2(arrived_ref[q, 0]), 1))
            total = total + nt(rows, jnp.concatenate(split2(spread_cols), 1))
        out_ref[...] = total - nt(left3(s_ref[...]), c3_ref[...])

    @pl.when((rng < jnp.minimum(c, PANELS)))
    def _():
        out_ref[...] = jnp.zeros_like(out_ref)

    for p, d_ref in enumerate((d0_ref, d1_ref, d2_ref)):
        @pl.when((c == p) & (rng > p))
        def _():
            out_ref[...] = s_ref[:, p * BLOCK : (p + 1) * BLOCK]

        @pl.when((c == p) & (rng == p))
        def _():
            pltpu.sync_copy(d_ref, out_ref)


def finish_call(place, row_rows, front, arrived, row_hot, col_hot, mats):
    return pl.pallas_call(
        finish,
        grid=(2,),
        in_specs=[
            SMEM,
            pl.BlockSpec((8, 1, BLOCK // 8, LEAD), lambda i: (0, i, 0, 0)),
            pl.BlockSpec((BLOCK, BLOCK), lambda i: (i, 0)),
            pl.BlockSpec((NKIDS, 1, PICK, PICK), lambda i: (0, i, 0, 0)),
            VMEM,
            VMEM,
        ]
        + [pl.BlockSpec(memory_space=pl.ANY)] * 10,
        out_specs=pl.BlockSpec((BLOCK, BLOCK), lambda i: (i, 0)),
        out_shape=jax.ShapeDtypeStruct(front.shape, F32),
        scratch_shapes=[
            pltpu.VMEM((3, BLOCK, 3 * BLOCK), B16),
            pltpu.VMEM((BLOCK, 3 * BLOCK), B16),
            pltpu.VMEM((BLOCK, 6 * BLOCK), B16),
            pltpu.VMEM((BLOCK, 9 * BLOCK), B16),
            pltpu.VMEM((BLOCK, LEAD), F32),
            pltpu.VMEM((BLOCK, LEAD), F32),
            pltpu.VMEM((6, BLOCK, BLOCK), F32),
            pltpu.VMEM((BLOCK, LEAD), F32),
            pltpu.SemaphoreType.DMA((7,)),
        ],
        compiler_params=PARAMS,
        cost_estimate=pl.CostEstimate(flops=20_000_000_000, bytes_accessed=24 << 20, transcendentals=0),
    )(place, row_rows, front, arrived, row_hot, col_hot, *mats)


ROW = ("x_hi", "z")
CHIP = ("y", "x_lo")
SHAPE = (2, 4, 4, 2, 2)
COL = CHIP + ("core",)


def copies_of(a, count):
    return jnp.broadcast_to(a[None], (count,) + a.shape)


def spread(a, axis, count):
    return lax.all_to_all(copies_of(a, count), axis, 0, 0, tiled=True)


def body(root_front, contrib, index_map):
    nr = lax.axis_size(ROW)
    nc = lax.axis_size(COL)
    r = lax.axis_index(ROW)
    c = lax.axis_index(COL)
    rows_loc, cols_loc = root_front.shape
    group = nr // NKIDS
    kid = r // group
    part = r % group
    per = cols_loc // nr
    stored = index_map.reshape(NKIDS, -1, PICK)
    index = stored - jnp.arange(CB // PICK, dtype=jnp.int32)[:, None] * BLOCK
    odd = lax.axis_index("core").reshape(1)

    def pick(kid_id, rng):
        return lax.dynamic_slice(stored, (kid_id, rng, 0), (1, 1, PICK)).reshape(1, PICK) - rng * BLOCK

    def swap(rows):
        return lax.ppermute(rows, "core", [(0, 1), (1, 0)])

    with jax.named_scope("slices"):
        outgoing = pl.pallas_call(
            prepare,
            grid=(1,),
            in_specs=[
                SMEM,
                VMEM,
                VMEM,
                pl.BlockSpec((2 * PICK, PICK), lambda i: (0, 0)),
                VMEM,
            ],
            out_specs=VMEM,
            out_shape=jax.ShapeDtypeStruct((cols_loc, 2 * BLOCK + PICK), F32),
            compiler_params=PARAMS,
        )(r.reshape(1), pick(kid, c), pick(kid, part), contrib, root_front)
        got = lax.all_to_all(outgoing.reshape(nr, per, -1), ROW, 0, 0, tiled=True)
        own_slice = pl.pallas_call(
            combine,
            in_specs=[VMEM, VMEM],
            out_specs=VMEM,
            out_shape=jax.ShapeDtypeStruct((per, LEAD), F32),
            compiler_params=SMALL,
        )(index[:, 2, :], got)

    with jax.named_scope("panel_cols"):
        far = lax.ppermute(own_slice, "x_hi", [(0, 1), (1, 0)])

    with jax.named_scope("lead"):
        pieces = lax.all_to_all(own_slice.reshape(nc // 2, per // (nc // 2), LEAD), CHIP, 0, 0, tiled=True)
        pieces, far, early = lax.optimization_barrier((pieces, far, own_slice))
        top, last = pieces[0], pieces[1]
        even_blocks = [top[:, :BLOCK], top[:, 2 * BLOCK :], last[:, 2 * BLOCK :]]
        odd_blocks = [top[:, BLOCK : 2 * BLOCK], top[:, :BLOCK], top[:, 2 * BLOCK :]]
        strip = jnp.where(odd[0] == 1, jnp.concatenate(odd_blocks, 1), jnp.concatenate(even_blocks, 1))
        both = jnp.concatenate([copies_of(strip, nr), pieces], 1)
        both = lax.all_to_all(both, ROW, 0, 0, tiled=True)
        strip = both[:, : pieces.shape[1]].reshape(-1, LEAD)
        share = both[:, pieces.shape[1] :].reshape(-1, LEAD)
        mine1 = spread(strip[:, :BLOCK], CHIP, nc // 2).reshape(-1, BLOCK)
        other1 = swap(mine1)
        fan = copies_of(strip[:, BLOCK:], nc // 2)
        mine1, other1, fan = lax.optimization_barrier((mine1, other1, fan))
        mine2 = lax.all_to_all(fan, CHIP, 0, 0, tiled=True).reshape(-1, 2 * BLOCK)

    with jax.named_scope("panel_cols"):
        high = lax.axis_index("x_hi") == 1
        pair = jnp.stack([jnp.where(high, far, early), jnp.where(high, early, far)])
        col_rows = lax.all_gather(pair, "z", axis=0, tiled=False)

    with jax.named_scope("factor"):
        square = pltpu.VMEM((BLOCK, BLOCK), F32)
        l00, w0 = factor_call(factor0, [SQUARE] * 2, [square], odd, mine1, other1)

    with jax.named_scope("panel_rows"):
        w0, share = lax.optimization_barrier((w0, share))
        row_rows = lax.all_gather(share, COL, axis=0, tiled=False)
        row_rows = row_rows.reshape(nc // 2, 2, per, LEAD)
        w0, contrib, mine2 = lax.optimization_barrier((w0, contrib, mine2))
        other2 = swap(mine2)

    with jax.named_scope("exchange"):
        arrived = lax.all_to_all(contrib.reshape(nr, PICK, PICK), ROW, 0, 0, tiled=True)

    with jax.named_scope("factor"):
        l11, w1, l10 = factor_call(
            factor1, [SQUARE] * 3, [square] * 2, odd, mine1, other1, mine2, other2, w0
        )
        l22, w2, l20, l21, solved = factor_call(
            factor2,
            [SQUARE] * 4 + [jax.ShapeDtypeStruct((cols_loc, LEAD), F32)],
            [square] * 3 + [pltpu.VMEM(col_rows.shape, F32), pltpu.SemaphoreType.DMA],
            odd, mine2, other2, w0, w1, l10, col_rows,
        )

    with jax.named_scope("finish"):
        mats = (w0, w1, w2, l10, l20, l21)
        row_hot = lax.dynamic_slice(index, (0, group * r, 0), (NKIDS, group, PICK)).transpose(1, 0, 2)
        col_hot = lax.dynamic_slice(index, (0, c, 0), (NKIDS, 1, PICK)).reshape(NKIDS, PICK)
        return finish_call(
            jnp.stack([r, c]),
            row_rows,
            root_front,
            arrived.reshape(NKIDS, group, PICK, PICK),
            row_hot,
            col_hot,
            (solved, *mats, l00, l11, l22),
        )


def solution(mesh):
    torus = Mesh(mesh.devices.reshape(SHAPE), ROW + COL)
    placed = (P(ROW, COL), P(ROW, COL), P())
    return jax.shard_map(
        body, mesh=torus, in_specs=placed, out_specs=P(ROW, COL), check_vma=False
    )
```

```python
import jax
import jax.numpy as jnp
from jax import lax
from jax.experimental import pallas as pl
from jax.experimental.pallas import tpu as pltpu
from jax.sharding import Mesh, PartitionSpec as P

CB = 4096
NKIDS = 4
BLOCK = 512
PANELS = 3
PICK = 256
LEAD = BLOCK * PANELS
F32 = jnp.float32
B16 = jnp.bfloat16


def split3(x):
    high = x.astype(B16).astype(F32)
    rest = x - high
    mid = rest.astype(B16).astype(F32)
    return high, mid, rest - mid


def outer_update(lhs, rhs):
    a_high, a_mid, a_low = split3(lhs)
    b_high, b_mid, b_low = split3(rhs)
    a = jnp.concatenate([a_high, a_high, a_mid, a_high, a_low, a_mid], 0).astype(B16)
    b = jnp.concatenate([b_high, b_mid, b_high, b_low, b_high, b_mid], 0).astype(B16)
    return lax.dot_general(a, b, (((0,), (0,)), ((), ())), preferred_element_type=F32)


def factor_tile(rows):
    count = len(rows)
    lane = lax.broadcasted_iota(jnp.int32, (8, 128), 1)
    sub = lax.broadcasted_iota(jnp.int32, (8, 128), 0)
    wide = lambda x: jnp.broadcast_to(x, (8, 128))
    rows = list(rows)
    uppers, inverses = [], []
    for k in range(count):
        c0 = 8 * k
        own = (lane >= c0) & (lane < c0 + 8)
        cur = rows[k]
        top = [wide(cur[:, c0 + j : c0 + j + 1]) for j in range(8)]
        near = range(k + 1, min(k + 3, count))
        lows = [[wide(rows[n][:, c0 + j : c0 + j + 1]) for j in range(8)] for n in near]
        afters = [jnp.where(own, 0.0, rows[n]) for n in near]
        upper = cur
        inv = jnp.where(own, jnp.where(lane - c0 == sub, 1.0, 0.0), cur)
        for j in range(8):
            scale = lax.rsqrt(wide(top[j][j : j + 1, :]))
            mult = jnp.where(sub > j, top[j] * scale, 0.0)
            low_mults = [low[j] * scale for low in lows]
            for m in range(j + 1, 8):
                u = wide(top[m][j : j + 1, :]) * scale
                top[m] = top[m] - mult * u
                for low, low_mult in zip(lows, low_mults):
                    low[m] = low[m] - low_mult * u
            u = wide(upper[j : j + 1, :]) * scale
            upper = jnp.where(sub == j, u, upper - mult * u)
            u = wide(inv[j : j + 1, :]) * scale
            inv = jnp.where(sub == j, u, inv - mult * u)
            afters = [after - low_mult * u for after, low_mult in zip(afters, low_mults)]
        uppers.append(jnp.where(lane - c0 >= sub, upper, 0.0))
        inverses.append(jnp.where(lane < c0 + 8, inv, 0.0))
        for n, after in zip(near, afters):
            rows[n] = after
        if k + 3 < count:
            update = outer_update(jnp.where(lane >= c0 + 24, upper, 0.0), inv)
            for i in range(k + 3, count):
                rows[i] = jnp.where(own, 0.0, rows[i]) - update[8 * i : 8 * i + 8, :]
    return uppers, inverses


def mm(a, b, flip=False):
    a_high, a_mid, a_low = (x.astype(B16) for x in split3(a))
    b_high, b_mid, b_low = (x.astype(B16) for x in split3(b))
    left = jnp.concatenate([a_high, a_high, a_mid, a_high, a_low, a_mid], 1)
    right = [b_high, b_mid, b_high, b_low, b_high, b_mid]
    if flip:
        return nt(left, jnp.concatenate(right, 1))
    return nn(left, jnp.concatenate(right, 0))


def nn(a, b):
    return lax.dot_general(a, b, (((1,), (0,)), ((), ())), preferred_element_type=F32)


def nt(a, b):
    return lax.dot_general(a, b, (((1,), (1,)), ((), ())), preferred_element_type=F32)


def split2(x):
    high = x.astype(B16)
    return high, (x - high.astype(F32)).astype(B16)


def left3(x):
    high, low = split2(x)
    return jnp.concatenate([high, high, low], 1)


def right3(x):
    high, low = split2(x)
    return jnp.concatenate([high, low, high], 1)


def mm3(a, b):
    return nt(left3(a), right3(b))


def whole(x):
    high, mid, low = split3(x)
    return jnp.concatenate([high, mid, low], 1).astype(B16)


def factor_block(l_ref, w_ref, s_ref):
    size = s_ref.shape[0]
    tiles = size // 128
    l_ref[...] = jnp.zeros_like(l_ref)
    w_ref[...] = jnp.zeros_like(w_ref)
    for k in range(tiles):
        o = 128 * k
        e = o + 128
        rows = [s_ref[o + 8 * i : o + 8 * i + 8, o:e] for i in range(16)]
        uppers, inverses = factor_tile(rows)
        inv = jnp.concatenate(inverses, 0)
        l_ref[o:e, o:e] = jnp.concatenate(uppers, 0).T
        w_ref[o:e, o:e] = inv
        if k + 1 < tiles:
            below = mm(s_ref[e:, o:e], inv, True)
            l_ref[e:, o:e] = below
            s_ref[e:, e:] = s_ref[e:, e:] - mm(below, below, True)
    half = 128
    while half < size:
        for o in range(0, size, 2 * half):
            m = o + half
            e = m + half
            t = mm(l_ref[m:e, o:m], w_ref[o:m, o:m])
            w_ref[m:e, o:m] = -mm(w_ref[m:e, m:e], t)
        half *= 2


def put_rows(dst, a_ref, b_ref, second, col):
    for q in range(8):
        for i in range(8):
            src = slice(64 * q + 8 * i, 64 * q + 8 * i + 8)
            cols = slice(col, col + BLOCK)
            dst[64 * i + 8 * q : 64 * i + 8 * q + 8, :] = jnp.where(second, b_ref[src, cols], a_ref[src, cols])


def factor0(odd_ref, mine_ref, other_ref, l_ref, w_ref, s_ref):
    put_rows(s_ref, mine_ref, other_ref, odd_ref[0] == 1, 0)
    factor_block(l_ref, w_ref, s_ref)


def factor1(odd_ref, mine1_ref, other1_ref, mine2_ref, other2_ref, w0_ref, l_ref, w_ref, l10_ref, s_ref, x_ref):
    even = odd_ref[0] == 0
    put_rows(x_ref, mine2_ref, other2_ref, even, 0)
    put_rows(s_ref, mine1_ref, other1_ref, even, 0)
    l10 = mm3(x_ref[...], w0_ref[...])
    l10_ref[...] = l10
    s_ref[...] = s_ref[...] - mm3(l10, l10)
    factor_block(l_ref, w_ref, s_ref)


def factor2(
    odd_ref, mine_ref, other_ref, w0_ref, w1_ref, l10_ref, cols_ref,
    l_ref, w_ref, l20_ref, l21_ref, solved_ref, s_ref, x_ref, y_ref, c_ref, sem,
):
    copy = pltpu.make_async_copy(cols_ref, c_ref, sem)
    copy.start()
    odd = odd_ref[0] == 1
    put_rows(x_ref, mine_ref, other_ref, odd, 0)
    put_rows(y_ref, mine_ref, other_ref, jnp.logical_not(odd), BLOCK)
    put_rows(s_ref, mine_ref, other_ref, odd, BLOCK)
    l20 = mm3(x_ref[...].T, w0_ref[...])
    l20_ref[...] = l20
    l21 = mm3(y_ref[...].T - mm3(l20, l10_ref[...]), w1_ref[...])
    l21_ref[...] = l21
    both = jnp.concatenate([l20, l21], 1)
    s_ref[...] = s_ref[...] - mm3(both, both)
    factor_block(l_ref, w_ref, s_ref)

    copy.wait()
    part = BLOCK // 8

    def rows(p):
        cols = slice(p * BLOCK, (p + 1) * BLOCK)
        for n in range(8):
            x_ref[n * part : (n + 1) * part, :] = c_ref[n % 4, n // 4, :, cols]
        return x_ref[...]

    s0 = mm3(rows(0), w0_ref[...])
    solved_ref[:, :BLOCK] = s0
    s1 = mm3(rows(1) - mm3(s0, l10_ref[...]), w1_ref[...])
    solved_ref[:, BLOCK : 2 * BLOCK] = s1
    early = mm3(s0, l20_ref[...]) + mm3(s1, l21_ref[...])
    solved_ref[:, 2 * BLOCK :] = mm3(rows(2) - early, w_ref[...])


VMEM = pl.BlockSpec(memory_space=pltpu.VMEM)
SMEM = pl.BlockSpec(memory_space=pltpu.SMEM)
PARAMS = pltpu.CompilerParams(vmem_limit_bytes=60 << 20)
SMALL = pltpu.CompilerParams(vmem_limit_bytes=16 << 20)


SQUARE = jax.ShapeDtypeStruct((BLOCK, BLOCK), F32)


def factor_call(kernel, outs, scratch, *args):
    specs = [pl.BlockSpec(memory_space=pl.ANY) if x.ndim > 2 else pl.BlockSpec(x.shape, lambda i: (0, 0)) for x in args[1:]]
    return pl.pallas_call(
        kernel,
        grid=(1,),
        in_specs=[SMEM] + specs,
        out_specs=[pl.BlockSpec(x.shape, lambda i: (0, 0)) for x in outs],
        out_shape=outs,
        scratch_shapes=scratch,
        compiler_params=PARAMS,
        cost_estimate=pl.CostEstimate(flops=20_000_000_000, bytes_accessed=1 << 24, transcendentals=0),
    )(*args)


def hot_t(index, size=BLOCK):
    place = lax.broadcasted_iota(jnp.int32, (size, index.shape[1]), 0)
    return (place == index).astype(F32).astype(B16)


def three(x):
    return jnp.concatenate([x, x, x], 1)


def prepare(flag_ref, cols_ref, rows_ref, contrib_ref, root_ref, out_ref):
    cols = three(hot_t(cols_ref[...]))
    rows = three(hot_t(rows_ref[...]))
    first = nt(whole(nt(cols, whole(contrib_ref[:PICK, :]))), rows)
    third = nt(cols, whole(contrib_ref[PICK:, :]))
    root_a = root_ref[:BLOCK, :].T
    root_b = root_ref[BLOCK:, :].T
    is_first = flag_ref[0] == 0
    out_ref[:, :BLOCK] = first + jnp.where(is_first, root_a, 0.0)
    out_ref[:, BLOCK : 2 * BLOCK] = jnp.where(is_first, root_b, root_a)
    out_ref[:, 2 * BLOCK :] = third


def combine(index_ref, got_ref, out_ref):
    first = lambda n: got_ref[n, :, :BLOCK]
    out_ref[:, :BLOCK] = (first(0) + first(2)) + (first(4) + first(6))
    out_ref[:, BLOCK : 2 * BLOCK] = (
        (first(1) + first(3)) + (first(5) + first(7)) + got_ref[0, :, BLOCK : 2 * BLOCK]
    )
    total = got_ref[1, :, BLOCK : 2 * BLOCK]
    for q in range(NKIDS):
        rows = three(hot_t(index_ref[q : q + 1, :]))
        total = total + nt(whole(got_ref[2 * q, :, 2 * BLOCK :]), rows)
    out_ref[:, 2 * BLOCK :] = total


def two(x):
    return jnp.concatenate([x, x], 1)


def finish(
    place_ref, rows_ref, front_ref, arrived_ref, row_hot_ref, col_hot_ref,
    solved_ref, w0_ref, w1_ref, w2_ref, l10_ref, l20_ref, l21_ref, d0_ref, d1_ref, d2_ref, out_ref, w3_ref, m10_ref, m2_ref, c3_ref, x_ref, s_ref, raw_ref, cols_ref, sem,
):
    step = pl.program_id(0)
    r = place_ref[0]
    c = place_ref[1]
    part = x_ref.shape[0] // 8
    sources = (w0_ref, l10_ref, w1_ref, l20_ref, l21_ref, w2_ref)
    copies = [
        pltpu.make_async_copy(src, raw_ref.at[n], sem.at[n]) for n, src in enumerate(sources)
    ] + [pltpu.make_async_copy(solved_ref, cols_ref, sem.at[len(sources)])]

    @pl.when(step == 0)
    def _():
        for copy in copies:
            copy.start()

    for q in range(8):
        for n in range(8):
            to = n * part + 8 * q
            x_ref[to : to + 8, :] = rows_ref[q, 0, 8 * n : 8 * n + 8, :]

    @pl.when(step == 0)
    def _():
        copies[0].wait()
        w3_ref[0] = right3(raw_ref[0])

    s_ref[:, :BLOCK] = nt(left3(x_ref[:, :BLOCK]), w3_ref[0])

    @pl.when(step == 0)
    def _():
        copies[1].wait()
        m10_ref[...] = right3(raw_ref[1])
        copies[2].wait()
        w3_ref[1] = right3(raw_ref[2])

    s1 = nt(left3(x_ref[:, BLOCK : 2 * BLOCK] - nt(left3(s_ref[:, :BLOCK]), m10_ref[...])), w3_ref[1])
    s_ref[:, BLOCK : 2 * BLOCK] = s1

    @pl.when(step == 0)
    def _():
        copies[3].wait()
        copies[4].wait()
        m2_ref[...] = right3(jnp.concatenate([raw_ref[3], raw_ref[4]], 1))
        copies[5].wait()
        w3_ref[2] = right3(raw_ref[5])

    s2 = nt(left3(x_ref[:, 2 * BLOCK :] - nt(left3(s_ref[:, : 2 * BLOCK]), m2_ref[...])), w3_ref[2])
    s_ref[:, 2 * BLOCK :] = s2

    @pl.when(step == 0)
    def _():
        copies[6].wait()
        c3_ref[...] = right3(cols_ref[...])

    rng = 2 * r + step

    @pl.when((c >= PANELS) & (rng >= PANELS))
    def _():
        total = front_ref[...]
        for q in range(NKIDS):
            cols = two(hot_t(col_hot_ref[q : q + 1, :]))
            rows = two(hot_t(row_hot_ref[step, q : q + 1, :]))
            spread_cols = nt(cols, jnp.concatenate(split2(arrived_ref[q, 0]), 1))
            total = total + nt(rows, jnp.concatenate(split2(spread_cols), 1))
        out_ref[...] = total - nt(left3(s_ref[...]), c3_ref[...])

    @pl.when((rng < jnp.minimum(c, PANELS)))
    def _():
        out_ref[...] = jnp.zeros_like(out_ref)

    for p, d_ref in enumerate((d0_ref, d1_ref, d2_ref)):
        @pl.when((c == p) & (rng > p))
        def _():
            out_ref[...] = s_ref[:, p * BLOCK : (p + 1) * BLOCK]

        @pl.when((c == p) & (rng == p))
        def _():
            pltpu.sync_copy(d_ref, out_ref)


def finish_call(place, row_rows, front, arrived, row_hot, col_hot, mats):
    return pl.pallas_call(
        finish,
        grid=(2,),
        in_specs=[
            SMEM,
            pl.BlockSpec((8, 1, BLOCK // 8, LEAD), lambda i: (0, i, 0, 0)),
            pl.BlockSpec((BLOCK, BLOCK), lambda i: (i, 0)),
            pl.BlockSpec((NKIDS, 1, PICK, PICK), lambda i: (0, i, 0, 0)),
            VMEM,
            VMEM,
        ]
        + [pl.BlockSpec(memory_space=pl.ANY)] * 10,
        out_specs=pl.BlockSpec((BLOCK, BLOCK), lambda i: (i, 0)),
        out_shape=jax.ShapeDtypeStruct(front.shape, F32),
        scratch_shapes=[
            pltpu.VMEM((3, BLOCK, 3 * BLOCK), B16),
            pltpu.VMEM((BLOCK, 3 * BLOCK), B16),
            pltpu.VMEM((BLOCK, 6 * BLOCK), B16),
            pltpu.VMEM((BLOCK, 9 * BLOCK), B16),
            pltpu.VMEM((BLOCK, LEAD), F32),
            pltpu.VMEM((BLOCK, LEAD), F32),
            pltpu.VMEM((6, BLOCK, BLOCK), F32),
            pltpu.VMEM((BLOCK, LEAD), F32),
            pltpu.SemaphoreType.DMA((7,)),
        ],
        compiler_params=PARAMS,
        cost_estimate=pl.CostEstimate(flops=20_000_000_000, bytes_accessed=24 << 20, transcendentals=0),
    )(place, row_rows, front, arrived, row_hot, col_hot, *mats)


ROW = ("x_hi", "z")
CHIP = ("y", "x_lo")
SHAPE = (2, 4, 4, 2, 2)
COL = CHIP + ("core",)


def copies_of(a, count):
    return jnp.broadcast_to(a[None], (count,) + a.shape)


def spread(a, axis, count):
    return lax.all_to_all(copies_of(a, count), axis, 0, 0, tiled=True)


def body(root_front, contrib, index_map):
    nr = lax.axis_size(ROW)
    nc = lax.axis_size(COL)
    r = lax.axis_index(ROW)
    c = lax.axis_index(COL)
    rows_loc, cols_loc = root_front.shape
    group = nr // NKIDS
    kid = r // group
    part = r % group
    per = cols_loc // nr
    stored = index_map.reshape(NKIDS, -1, PICK)
    index = stored - jnp.arange(CB // PICK, dtype=jnp.int32)[:, None] * BLOCK
    odd = lax.axis_index("core").reshape(1)

    def pick(kid_id, rng):
        return lax.dynamic_slice(stored, (kid_id, rng, 0), (1, 1, PICK)).reshape(1, PICK) - rng * BLOCK

    def swap(rows):
        return lax.ppermute(rows, "core", [(0, 1), (1, 0)])

    with jax.named_scope("slices"):
        outgoing = pl.pallas_call(
            prepare,
            grid=(1,),
            in_specs=[
                SMEM,
                VMEM,
                VMEM,
                pl.BlockSpec((2 * PICK, PICK), lambda i: (0, 0)),
                VMEM,
            ],
            out_specs=VMEM,
            out_shape=jax.ShapeDtypeStruct((cols_loc, 2 * BLOCK + PICK), F32),
            compiler_params=PARAMS,
        )(r.reshape(1), pick(kid, c), pick(kid, part), contrib, root_front)
        got = lax.all_to_all(outgoing.reshape(nr, per, -1), ROW, 0, 0, tiled=True)
        own_slice = pl.pallas_call(
            combine,
            in_specs=[VMEM, VMEM],
            out_specs=VMEM,
            out_shape=jax.ShapeDtypeStruct((per, LEAD), F32),
            compiler_params=SMALL,
        )(index[:, 2, :], got)

    with jax.named_scope("panel_cols"):
        far = lax.ppermute(own_slice, "x_hi", [(0, 1), (1, 0)])

    with jax.named_scope("lead"):
        pieces = lax.all_to_all(own_slice.reshape(nc // 2, per // (nc // 2), LEAD), CHIP, 0, 0, tiled=True)
        pieces, far, early = lax.optimization_barrier((pieces, far, own_slice))
        top, last = pieces[0], pieces[1]
        even_blocks = [top[:, :BLOCK], top[:, 2 * BLOCK :], last[:, 2 * BLOCK :]]
        odd_blocks = [top[:, BLOCK : 2 * BLOCK], top[:, :BLOCK], top[:, 2 * BLOCK :]]
        strip = jnp.where(odd[0] == 1, jnp.concatenate(odd_blocks, 1), jnp.concatenate(even_blocks, 1))
        both = jnp.concatenate([copies_of(strip, nr), pieces], 1)
        both = lax.all_to_all(both, ROW, 0, 0, tiled=True)
        strip = both[:, : pieces.shape[1]].reshape(-1, LEAD)
        share = both[:, pieces.shape[1] :].reshape(-1, LEAD)
        mine1 = spread(strip[:, :BLOCK], CHIP, nc // 2).reshape(-1, BLOCK)
        other1 = swap(mine1)
        fan = copies_of(strip[:, BLOCK:], nc // 2)
        mine1, other1, fan = lax.optimization_barrier((mine1, other1, fan))
        mine2 = lax.all_to_all(fan, CHIP, 0, 0, tiled=True).reshape(-1, 2 * BLOCK)

    with jax.named_scope("panel_cols"):
        high = lax.axis_index("x_hi") == 1
        pair = jnp.stack([jnp.where(high, far, early), jnp.where(high, early, far)])
        col_rows = lax.all_gather(pair, "z", axis=0, tiled=False)

    with jax.named_scope("factor"):
        square = pltpu.VMEM((BLOCK, BLOCK), F32)
        l00, w0 = factor_call(factor0, [SQUARE] * 2, [square], odd, mine1, other1)

    with jax.named_scope("panel_rows"):
        w0, contrib, mine2, share = lax.optimization_barrier((w0, contrib, mine2, share))
        other2 = swap(mine2)
        row_rows = lax.all_gather(share, COL, axis=0, tiled=False)
        row_rows = row_rows.reshape(nc // 2, 2, per, LEAD)

    with jax.named_scope("exchange"):
        arrived = lax.all_to_all(contrib.reshape(nr, PICK, PICK), ROW, 0, 0, tiled=True)

    with jax.named_scope("factor"):
        l11, w1, l10 = factor_call(
            factor1, [SQUARE] * 3, [square] * 2, odd, mine1, other1, mine2, other2, w0
        )
        l22, w2, l20, l21, solved = factor_call(
            factor2,
            [SQUARE] * 4 + [jax.ShapeDtypeStruct((cols_loc, LEAD), F32)],
            [square] * 3 + [pltpu.VMEM(col_rows.shape, F32), pltpu.SemaphoreType.DMA],
            odd, mine2, other2, w0, w1, l10, col_rows,
        )

    with jax.named_scope("finish"):
        mats = (w0, w1, w2, l10, l20, l21)
        row_hot = lax.dynamic_slice(index, (0, group * r, 0), (NKIDS, group, PICK)).transpose(1, 0, 2)
        col_hot = lax.dynamic_slice(index, (0, c, 0), (NKIDS, 1, PICK)).reshape(NKIDS, PICK)
        return finish_call(
            jnp.stack([r, c]),
            row_rows,
            root_front,
            arrived.reshape(NKIDS, group, PICK, PICK),
            row_hot,
            col_hot,
            (solved, *mats, l00, l11, l22),
        )


def solution(mesh):
    torus = Mesh(mesh.devices.reshape(SHAPE), ROW + COL)
    placed = (P(ROW, COL), P(ROW, COL), P())
    return jax.shard_map(
        body, mesh=torus, in_specs=placed, out_specs=P(ROW, COL), check_vma=False
    )
```
